32 devices in a mesh: row: 16 (over z, y, x), col: 2 (over core).
Axes of the slice: x: 2, y: 2, z: 4, core: 2. Of those that a mesh axis runs over, the one named last changes fastest.
Arguments:
- density: bfloat16 [256, 64, 1024], P('row', None, 'col'), may hold values from -0.9 to 1.9
- columns: int32 [256, 16], replicated, may hold values from 0 to 255, as said below
Outputs:
- purified: float32 [256, 64, 1024], P('row', None, 'col')
The draws below stay inside these ranges and needn't reach their ends.
Inputs may be any that keep to these rules, and one draw needn't show every extreme that they name: Stored block a of row i lies in group a // 8: columns[i, a] is congruent to a // 8 modulo 2. The columns of a row are distinct and lie within cyclic distance 48 of i; row 0 always stores a block at distance exactly 48, and other rows may as well. The diagonal column i stands in slot (i mod 2) * 8.
All inputs are finite; a program needn't handle non-finite values.
Results may differ from the reference program's by a relative error of at most 0.0034.
Values may be sent and summed in bfloat16 or wider, within the bound.
A program may use at most 128 MiB of HBM per device.

```python
import jax
import jax.numpy as jnp
from jax import lax

B = 64
K = 16
R_DEV = 16
NB = 256
H = 48
GROUPS = 2
K_G = 8


def draw_columns(key, part):
    key = jax.random.fold_in(key, 11)
    count = (2 * H + 1) // GROUPS
    rows = jnp.arange(NB, dtype=jnp.int32)[:, None, None]
    groups = jnp.arange(GROUPS, dtype=jnp.int32)[None, :, None]
    steps = jnp.arange(count, dtype=jnp.int32)[None, None, :]
    first = jnp.mod(groups - rows + H, GROUPS) - H
    offsets = first + steps * GROUPS
    scores = jax.random.randint(key, (NB, GROUPS, count), 0, 1 << 20, dtype=jnp.int32) * count + steps
    scores = jnp.where(offsets == 0, -2, scores)
    scores = jnp.where((rows == 0) & (offsets == -H), -1, scores)
    order = jnp.argsort(scores, axis=-1)[..., :K_G]
    picked = jnp.take_along_axis(offsets, order, axis=-1)
    return jnp.mod(rows + picked, NB).reshape(NB, K).astype(jnp.int32)


def draw_density(key, part):
    key = jax.random.fold_in(key, 23)
    noise_key, fill_key = jax.random.split(key)
    noise = jnp.clip(0.15 * jax.random.normal(noise_key, (NB, B, K * B), jnp.float32), -0.9, 0.9)
    occupation = jax.random.uniform(fill_key, (NB, B, 1), jnp.float32, 0.0, 1.0)
    rows = jnp.arange(NB, dtype=jnp.int32)[:, None, None]
    line = jnp.arange(B, dtype=jnp.int32)[None, :, None]
    column = jnp.arange(K * B, dtype=jnp.int32)[None, None, :]
    target = jnp.mod(rows, GROUPS) * K_G * B + line
    return (noise + jnp.where(column == target, occupation, 0.0)).astype(jnp.bfloat16)


def setup_inputs(seed: int = 0) -> dict:
    streams_of = jax.random.split(jax.random.key(seed), 3)
    return {
        "density": draw_density(jax.random.fold_in(streams_of[2], 71), 0),
        "columns": draw_columns(jax.random.fold_in(streams_of[2], 71), 0),
    }


def to_blocks(values, count, width):
    return values.reshape(values.shape[0], width, count, width).transpose(0, 2, 1, 3)


def product(left, right, columns):
    count = columns.shape[1]
    width = left.shape[1]
    total = columns.shape[0]
    left_blocks = to_blocks(left, count, width).astype(jnp.float32)
    right_blocks = to_blocks(right, count, width).astype(jnp.float32)
    candidates = columns[columns]
    equal = candidates[:, None, :, :] == columns[:, :, None, None]
    live = jnp.any(equal, axis=-1)
    slots = jnp.arange(count, dtype=jnp.int32)
    chosen_slot = jnp.sum(jnp.where(equal, slots, 0), axis=-1).astype(jnp.int32)
    batches = total // R_DEV

    def one_batch(pieces):
        left_part, inner_rows, slot_part, live_part = pieces
        taken = right_blocks[inner_rows[:, None, :], slot_part]
        taken = jnp.where(live_part[..., None, None], taken, 0.0)
        return jnp.einsum("ibxy,iabyz->iaxz", left_part, taken)

    result = lax.map(one_batch, (left_blocks.reshape(batches, R_DEV, count, width, width),
                                 columns.reshape(batches, R_DEV, count),
                                 chosen_slot.reshape(batches, R_DEV, count, count),
                                 live.reshape(batches, R_DEV, count, count)))
    result = result.reshape(total, count, width, width)
    return result.transpose(0, 2, 1, 3).reshape(total, width, count * width)


def reference(density, columns):
    square = product(density, density, columns).astype(jnp.bfloat16)
    cube = product(square, density, columns)
    return 3.0 * square.astype(jnp.float32) - 2.0 * cube
```

```python
import functools

import jax
import jax.numpy as jnp
from jax import lax
from jax.experimental import pallas as pl
from jax.experimental.pallas import tpu as pltpu
from jax.sharding import PartitionSpec as P

REACH = 48
UNROLL = 4


def passed_along(block, axis, distance):
    size = lax.axis_size(axis)
    route = [((i - distance) % size, i) for i in range(size)]
    return lax.ppermute(block, axis, route)


def live_list(columns, rows, width, group_size, span):
    total, stored = columns.shape
    base = lax.axis_index("row") * rows
    first = lax.axis_index("col") * group_size
    own = lax.dynamic_slice_in_dim(columns, base, rows, 0)
    wanted = lax.dynamic_slice_in_dim(own, first, group_size, 1)
    group = lax.dynamic_slice_in_dim(columns, first, group_size, 1)
    candidates = jnp.take(group, own, axis=0)
    distance = jnp.mod(own - base + span * rows, total)
    equal = candidates[:, :, :, None] == wanted[:, None, None, :]
    slots = jnp.arange(group_size, dtype=jnp.int32)
    live = jnp.any(equal, axis=-1)
    place = jnp.sum(jnp.where(equal, slots, 0), axis=-1)
    inner = jnp.arange(stored, dtype=jnp.int32)[None, :, None]
    code = ((distance[:, :, None] * group_size + slots) * stored + inner) * group_size + place
    flat = live.reshape(rows, stored * group_size)
    code = code.reshape(rows, stored * group_size)
    order = jnp.cumsum(flat.astype(jnp.int32), axis=1)
    ranks = jnp.arange(1, stored * group_size + 1, dtype=jnp.int32)
    chosen = flat[:, None, :] & (order[:, None, :] == ranks[None, :, None])
    packed = jnp.sum(jnp.where(chosen, code[:, None, :] + 1, 0), axis=-1)
    return order[:, -1], packed - 1


def first_kernel(stored, group_size, width, count_ref, code_ref, panels_ref, left_ref, right_ref, square_ref):
    row = pl.program_id(0)
    right_ref[...] = jnp.zeros_like(right_ref)
    half = lax.broadcasted_iota(jnp.int32, (width, 2 * width), 1) >= width

    def one(entry, carry):
        pieces = []
        for part in range(UNROLL):
            raw = code_ref[row, entry * UNROLL + part]
            real = raw >= 0
            code = jnp.maximum(raw, 0)
            place = lax.rem(code, group_size)
            code = lax.div(code, group_size)
            inner = lax.rem(code, stored)
            code = lax.div(code, stored)
            slot = lax.rem(code, group_size)
            source = lax.div(code, group_size)
            lanes = pl.ds(pl.multiple_of(lax.div(slot, 2) * 2 * width, 2 * width), 2 * width)
            value = panels_ref[source, :, lanes]
            swapped = jnp.concatenate([value[:, width:], value[:, :width]], axis=1)
            odd = lax.rem(place, 2)
            same = jnp.full(value.shape, lax.rem(slot, 2), jnp.int32) == odd
            value = jnp.where(same, value, swapped)
            mine = (half == (jnp.full(value.shape, odd, jnp.int32) == 1)) & jnp.full(value.shape, real)
            pieces.append((inner, place, jnp.where(mine, value, jnp.zeros_like(value))))
        for inner, place, value in pieces:
            lanes = pl.ds(pl.multiple_of(lax.div(place, 2) * 2 * width, 2 * width), 2 * width)
            lines = pl.ds(pl.multiple_of(inner * width, width), width)
            right_ref[0, lines, lanes] += value
        return carry

    lax.fori_loop(0, lax.div(count_ref[row] + UNROLL - 1, UNROLL), one, 0)
    total = None
    depth = group_size * width
    for group in range(left_ref.shape[0]):
        part = jnp.dot(
            left_ref[group, 0], right_ref[0, group * depth:(group + 1) * depth, :],
            preferred_element_type=jnp.float32,
        )
        total = part if total is None else total + part
    square_ref[0] = total.astype(square_ref.dtype)


def second_kernel(left_ref, right_ref, square_ref, out_ref):
    total = None
    depth = left_ref.shape[3]
    for group in range(left_ref.shape[0]):
        part = jnp.dot(
            left_ref[group, 0], right_ref[0, group * depth:(group + 1) * depth, :],
            preferred_element_type=jnp.float32,
        )
        total = part if total is None else total + part
    out_ref[0] = 3.0 * square_ref[0].astype(jnp.float32) - 2.0 * total


def shards(density, columns):
    rows, width, depth = density.shape
    total, stored = columns.shape
    group_size = depth // width
    groups = stored // group_size
    span = -(-REACH // rows)
    count, codes = live_list(columns, rows, width, group_size, span)
    panels = [
        density if offset == 0 else passed_along(density, "row", -offset)
        for offset in range(-span, span + 1)
    ]
    panels = jnp.concatenate(panels, axis=0)
    left = lax.all_gather(density, "col", axis=0)
    left_spec = pl.BlockSpec((groups, 1, width, depth), lambda i, *_: (0, i, 0, 0))
    right_spec = pl.BlockSpec((1, stored * width, depth), lambda i, *_: (i, 0, 0))
    row_spec = pl.BlockSpec((1, width, depth), lambda i, *_: (i, 0, 0))
    right, square = pl.pallas_call(
        functools.partial(first_kernel, stored, group_size, width),
        grid_spec=pltpu.PrefetchScalarGridSpec(
            num_scalar_prefetch=2,
            grid=(rows,),
            in_specs=[pl.BlockSpec(panels.shape, lambda i, *_: (0, 0, 0)), left_spec],
            out_specs=[right_spec, row_spec],
        ),
        out_shape=[
            jax.ShapeDtypeStruct((rows, stored * width, depth), density.dtype),
            jax.ShapeDtypeStruct(density.shape, density.dtype),
        ],
        compiler_params=pltpu.CompilerParams(vmem_limit_bytes=40 * 1024 * 1024),
    )(count, codes, panels, left)
    gathered = lax.all_gather(square, "col", axis=0)
    return pl.pallas_call(
        second_kernel,
        grid=(rows,),
        in_specs=[left_spec, right_spec, row_spec],
        out_specs=row_spec,
        out_shape=jax.ShapeDtypeStruct(density.shape, jnp.float32),
        compiler_params=pltpu.CompilerParams(vmem_limit_bytes=40 * 1024 * 1024),
    )(gathered, right, square)


def solution(mesh):
    placed = (P("row", None, "col"), P())
    return jax.shard_map(
        shards, mesh=mesh, in_specs=placed, out_specs=P("row", None, "col"), check_vma=False
    )
```

```python
import functools

import jax
import jax.numpy as jnp
from jax import lax
from jax.experimental import pallas as pl
from jax.experimental.pallas import tpu as pltpu
from jax.sharding import PartitionSpec as P

REACH = 48
UNROLL = 4


def greet(devices):
    barrier = pltpu.get_barrier_semaphore()
    for device in devices:
        pl.semaphore_signal(barrier, inc=1, device_id=device, device_id_type=pl.DeviceIdType.MESH)
    pl.semaphore_wait(barrier, len(devices))


def col_peers(groups):
    return [{"col": lax.rem(lax.axis_index("col") + step, groups)} for step in range(1, groups)]


def share_with_peers(groups, block, shared, local_sem, send_sem, recv_sem):
    here = lax.axis_index("col")
    local = pltpu.make_async_copy(block, shared.at[here], local_sem)
    local.start()
    copies = []
    for step, peer in enumerate(col_peers(groups)):
        copies.append(pltpu.make_async_remote_copy(
            src_ref=block, dst_ref=shared.at[here], send_sem=send_sem.at[step], recv_sem=recv_sem.at[step],
            device_id=peer, device_id_type=pl.DeviceIdType.MESH,
        ))
        copies[-1].start()
    return local, copies


def exchange_kernel(groups, block, shared, local_sem, send_sem, recv_sem):
    greet(col_peers(groups))
    local, copies = share_with_peers(groups, block, shared, local_sem, send_sem, recv_sem)
    for copy in copies:
        copy.wait()
    local.wait()


def exchange(block, groups, collective_id):
    return pl.pallas_call(
        functools.partial(exchange_kernel, groups),
        in_specs=[pl.BlockSpec(memory_space=pl.ANY)],
        out_specs=pl.BlockSpec(memory_space=pl.ANY),
        out_shape=jax.ShapeDtypeStruct((groups,) + block.shape, block.dtype),
        scratch_shapes=[
            pltpu.SemaphoreType.DMA,
            pltpu.SemaphoreType.DMA((groups - 1,)),
            pltpu.SemaphoreType.DMA((groups - 1,)),
        ],
        compiler_params=pltpu.CompilerParams(collective_id=collective_id, has_side_effects=True),
    )(block)


def direct_kernel(groups, size, span, block, panels, shared, own_sem, local_sem, col_send, col_recv, send_sem, recv_sem):
    me = lax.axis_index("row")
    offsets = [d for d in range(-span, span + 1) if d != 0]
    greet([{"row": lax.rem(me + d + size, size)} for d in offsets] + col_peers(groups))
    own = pltpu.make_async_copy(block, panels.at[span], own_sem)
    own.start()
    local, copies = share_with_peers(groups, block, shared, local_sem, col_send, col_recv)
    for step, d in enumerate(offsets):
        copies.append(pltpu.make_async_remote_copy(
            src_ref=block, dst_ref=panels.at[span - d], send_sem=send_sem.at[step], recv_sem=recv_sem.at[step],
            device_id={"row": lax.rem(me + d + size, size)}, device_id_type=pl.DeviceIdType.MESH,
        ))
        copies[-1].start()
    for copy in copies:
        copy.wait()
    local.wait()
    own.wait()


def relay_kernel(groups, size, chunks, block, panels, shared, own_sem, local_sem, col_send, col_recv, send_sem, recv_sem):
    me = lax.axis_index("row")
    x_step = 1 - 2 * lax.rem(me, 2)
    y_step = 2 - 4 * lax.rem(lax.div(me, 2), 2)
    steps = [x_step, y_step, x_step + y_step]
    x_near, y_near = me + x_step, me + y_step
    above, below = lax.rem(me + 4, size), lax.rem(me + size - 4, size)
    greet([{"row": d} for d in (x_near, y_near, above, below)] + col_peers(groups))
    own = pltpu.make_async_copy(block, panels.at[3], own_sem)
    own.start()
    local, others = share_with_peers(groups, block, shared, local_sem, col_send, col_recv)
    depth = block.shape[0] // chunks

    def send(kind, chunk, source, slot, device):
        lines = pl.ds(chunk * depth, depth)
        copy = pltpu.make_async_remote_copy(
            src_ref=source.at[lines], dst_ref=panels.at[slot, lines],
            send_sem=send_sem.at[kind, chunk], recv_sem=recv_sem.at[kind, chunk],
            device_id={"row": device}, device_id_type=pl.DeviceIdType.MESH,
        )
        copy.start()
        others.append(copy)
        return copy

    def pass_on(kind, chunk):
        step = steps[kind]
        sign = jnp.where(step > 0, 1, -1)
        target = lax.rem(me + 4 * sign + size, size)
        late.append(send(3 + kind, chunk, panels.at[3 + step], 3 + step - 4 * sign, target))

    late, arriving = [], []
    for chunk in range(chunks):
        arriving.append((
            send(0, chunk, block, 3 - x_step, x_near),
            send(1, chunk, block, 3 - y_step, y_near),
        ))
    corner = []
    lag = 2
    for chunk in range(chunks + lag):
        if chunk < chunks:
            arriving[chunk][0].wait_recv()
            if chunk % 2 == 0:
                corner.append(send(2, chunk, panels.at[3 + x_step], 3 + x_step - y_step, y_near))
            pass_on(0, chunk)
            arriving[chunk][1].wait_recv()
            if chunk % 2 == 1:
                corner.append(send(2, chunk, panels.at[3 + y_step], 3 + y_step - x_step, x_near))
            pass_on(1, chunk)
        if chunk >= lag:
            corner[chunk - lag].wait_recv()
            pass_on(2, chunk - lag)
    for copy in late:
        copy.wait_recv()
    for copy in others[:groups - 1]:
        copy.wait_recv()
    for copy in others:
        copy.wait_send()
    local.wait()
    own.wait()


def fetch(density, groups, size, span, planes):
    chunks = 8
    if planes:
        body, shape = functools.partial(relay_kernel, groups, size, chunks), (6, chunks)
    else:
        body, shape = functools.partial(direct_kernel, groups, size, span), (2 * span,)
    anywhere = pl.BlockSpec(memory_space=pl.ANY)
    panels, shared = pl.pallas_call(
        body,
        in_specs=[anywhere],
        out_specs=[anywhere, anywhere],
        out_shape=[
            jax.ShapeDtypeStruct((2 * span + 1,) + density.shape, density.dtype),
            jax.ShapeDtypeStruct((groups,) + density.shape, density.dtype),
        ],
        scratch_shapes=[
            pltpu.SemaphoreType.DMA,
            pltpu.SemaphoreType.DMA,
            pltpu.SemaphoreType.DMA((groups - 1,)),
            pltpu.SemaphoreType.DMA((groups - 1,)),
            pltpu.SemaphoreType.DMA(shape),
            pltpu.SemaphoreType.DMA(shape),
        ],
        compiler_params=pltpu.CompilerParams(collective_id=0, has_side_effects=True),
    )(density)
    return panels.reshape((-1,) + density.shape[1:]), shared


def live_list(columns, rows, width, group_size, span):
    total, stored = columns.shape
    base = lax.axis_index("row") * rows
    first = lax.axis_index("col") * group_size
    own = lax.dynamic_slice_in_dim(columns, base, rows, 0)
    wanted = lax.dynamic_slice_in_dim(own, first, group_size, 1)
    group = lax.dynamic_slice_in_dim(columns, first, group_size, 1)
    candidates = jnp.take(group, own, axis=0)
    distance = jnp.mod(own - base + span * rows, total)
    equal = candidates[:, :, :, None] == wanted[:, None, None, :]
    slots = jnp.arange(group_size, dtype=jnp.int32)
    live = jnp.any(equal, axis=-1)
    place = jnp.sum(jnp.where(equal, slots, 0), axis=-1)
    inner = jnp.arange(stored, dtype=jnp.int32)[None, :, None]
    code = ((distance[:, :, None] * group_size + slots) * stored + inner) * group_size + place
    flat = live.reshape(rows, stored * group_size)
    code = code.reshape(rows, stored * group_size)
    order = jnp.cumsum(flat.astype(jnp.int32), axis=1)
    ranks = jnp.arange(1, stored * group_size + 1, dtype=jnp.int32)
    chosen = flat[:, None, :] & (order[:, None, :] == ranks[None, :, None])
    packed = jnp.sum(jnp.where(chosen, code[:, None, :] + 1, 0), axis=-1)
    return order[:, -1], packed - 1


def first_kernel(stored, group_size, width, count_ref, code_ref, panels_ref, left_ref, right_ref, square_ref):
    row = pl.program_id(0)
    right_ref[...] = jnp.zeros_like(right_ref)
    half = lax.broadcasted_iota(jnp.int32, (width, 2 * width), 1) >= width

    def one(entry, carry):
        pieces = []
        for part in range(UNROLL):
            raw = code_ref[row, entry * UNROLL + part]
            real = raw >= 0
            code = jnp.maximum(raw, 0)
            place = lax.rem(code, group_size)
            code = lax.div(code, group_size)
            inner = lax.rem(code, stored)
            code = lax.div(code, stored)
            slot = lax.rem(code, group_size)
            source = lax.div(code, group_size)
            lanes = pl.ds(pl.multiple_of(lax.div(slot, 2) * 2 * width, 2 * width), 2 * width)
            value = panels_ref[source, :, lanes]
            swapped = jnp.concatenate([value[:, width:], value[:, :width]], axis=1)
            odd = lax.rem(place, 2)
            same = jnp.full(value.shape, lax.rem(slot, 2), jnp.int32) == odd
            value = jnp.where(same, value, swapped)
            mine = (half == (jnp.full(value.shape, odd, jnp.int32) == 1)) & jnp.full(value.shape, real)
            pieces.append((inner, place, jnp.where(mine, value, jnp.zeros_like(value))))
        for inner, place, value in pieces:
            lanes = pl.ds(pl.multiple_of(lax.div(place, 2) * 2 * width, 2 * width), 2 * width)
            lines = pl.ds(pl.multiple_of(inner * width, width), width)
            right_ref[0, lines, lanes] += value
        return carry

    lax.fori_loop(0, lax.div(count_ref[row] + UNROLL - 1, UNROLL), one, 0)
    total = None
    depth = group_size * width
    for group in range(left_ref.shape[0]):
        part = jnp.dot(
            left_ref[group, 0], right_ref[0, group * depth:(group + 1) * depth, :],
            preferred_element_type=jnp.float32,
        )
        total = part if total is None else total + part
    square_ref[0] = total.astype(square_ref.dtype)


def second_kernel(left_ref, right_ref, square_ref, out_ref):
    total = None
    depth = left_ref.shape[3]
    for group in range(left_ref.shape[0]):
        part = jnp.dot(
            left_ref[group, 0], right_ref[0, group * depth:(group + 1) * depth, :],
            preferred_element_type=jnp.float32,
        )
        total = part if total is None else total + part
    out_ref[0] = 3.0 * square_ref[0].astype(jnp.float32) - 2.0 * total


def shards(density, columns):
    rows, width, depth = density.shape
    total, stored = columns.shape
    group_size = depth // width
    groups = stored // group_size
    span = -(-REACH // rows)
    count, codes = live_list(columns, rows, width, group_size, span)
    size = lax.axis_size("row")
    planes = (size, groups, span) == (16, 2, 3)
    panels, left = fetch(density, groups, size, span, planes)
    left_spec = pl.BlockSpec((groups, 1, width, depth), lambda i, *_: (0, i, 0, 0))
    right_spec = pl.BlockSpec((1, stored * width, depth), lambda i, *_: (i, 0, 0))
    row_spec = pl.BlockSpec((1, width, depth), lambda i, *_: (i, 0, 0))
    right, square = pl.pallas_call(
        functools.partial(first_kernel, stored, group_size, width),
        grid_spec=pltpu.PrefetchScalarGridSpec(
            num_scalar_prefetch=2,
            grid=(rows,),
            in_specs=[pl.BlockSpec(panels.shape, lambda i, *_: (0, 0, 0)), left_spec],
            out_specs=[right_spec, row_spec],
        ),
        out_shape=[
            jax.ShapeDtypeStruct((rows, stored * width, depth), density.dtype),
            jax.ShapeDtypeStruct(density.shape, density.dtype),
        ],
        compiler_params=pltpu.CompilerParams(vmem_limit_bytes=40 * 1024 * 1024),
    )(count, codes, panels, left)
    gathered = exchange(square, groups, 1)
    return pl.pallas_call(
        second_kernel,
        grid=(rows,),
        in_specs=[left_spec, right_spec, row_spec],
        out_specs=row_spec,
        out_shape=jax.ShapeDtypeStruct(density.shape, jnp.float32),
        compiler_params=pltpu.CompilerParams(vmem_limit_bytes=40 * 1024 * 1024),
    )(gathered, right, square)


def solution(mesh):
    placed = (P("row", None, "col"), P())
    return jax.shard_map(
        shards, mesh=mesh, in_specs=placed, out_specs=P("row", None, "col"), check_vma=False
    )
```

```python
import functools

import jax
import jax.numpy as jnp
from jax import lax
from jax.experimental import pallas as pl
from jax.experimental.pallas import tpu as pltpu
from jax.sharding import PartitionSpec as P

REACH = 48
UNROLL = 4
PIECES = 8


def greet(devices):
    barrier = pltpu.get_barrier_semaphore()
    for device in devices:
        pl.semaphore_signal(barrier, inc=1, device_id=device, device_id_type=pl.DeviceIdType.MESH)
    pl.semaphore_wait(barrier, len(devices))


def col_peers(groups):
    return [{"col": lax.rem(lax.axis_index("col") + step, groups)} for step in range(1, groups)]


def share_with_peers(groups, block, shared, send_sem, recv_sem):
    copies = []
    chunks = send_sem.shape[1]
    depth = block.shape[0] // chunks
    for step, peer in enumerate(col_peers(groups)):
        for chunk in range(chunks):
            lines = pl.ds(chunk * depth, depth)
            copies.append(pltpu.make_async_remote_copy(
                src_ref=block.at[lines], dst_ref=shared.at[groups - 2 - step, lines],
                send_sem=send_sem.at[step, chunk], recv_sem=recv_sem.at[step, chunk],
                device_id=peer, device_id_type=pl.DeviceIdType.MESH,
            ))
            copies[-1].start()
    return copies


def exchange_kernel(groups, block, shared, send_sem, recv_sem):
    greet(col_peers(groups))
    for copy in share_with_peers(groups, block, shared, send_sem, recv_sem):
        copy.wait()


def exchange(block, groups, collective_id):
    return pl.pallas_call(
        functools.partial(exchange_kernel, groups),
        in_specs=[pl.BlockSpec(memory_space=pl.ANY)],
        out_specs=pl.BlockSpec(memory_space=pl.ANY),
        out_shape=jax.ShapeDtypeStruct((groups - 1,) + block.shape, block.dtype),
        scratch_shapes=[pltpu.SemaphoreType.DMA((groups - 1, PIECES))] * 2,
        compiler_params=pltpu.CompilerParams(collective_id=collective_id, has_side_effects=True),
    )(block)


def turn(block, turned, pair):
    wide = jnp.concatenate([block[2 * pair], block[2 * pair + 1]], axis=0)
    turned[pair] = wide.T


def direct_kernel(groups, size, span, block, panels, shared, turned, own_sem, col_send, col_recv, send_sem, recv_sem):
    me = lax.axis_index("row")
    offsets = [d for d in range(-span, span + 1) if d != 0]
    greet([{"row": lax.rem(me + d + size, size)} for d in offsets] + col_peers(groups))
    copies = share_with_peers(groups, block, shared, col_send, col_recv)
    for pair in range(turned.shape[0]):
        turn(block, turned, pair)
    own = pltpu.make_async_copy(turned, panels.at[span], own_sem)
    own.start()
    for step, d in enumerate(offsets):
        copies.append(pltpu.make_async_remote_copy(
            src_ref=turned, dst_ref=panels.at[span - d], send_sem=send_sem.at[step], recv_sem=recv_sem.at[step],
            device_id={"row": lax.rem(me + d + size, size)}, device_id_type=pl.DeviceIdType.MESH,
        ))
        copies[-1].start()
    for copy in copies:
        copy.wait()
    own.wait()


def relay_kernel(groups, size, chunks, block, panels, shared, turned, own_sem, col_send, col_recv, send_sem, recv_sem):
    me = lax.axis_index("row")
    x_step = 1 - 2 * lax.rem(me, 2)
    y_step = 2 - 4 * lax.rem(lax.div(me, 2), 2)
    steps = [x_step, y_step, x_step + y_step]
    x_near, y_near = me + x_step, me + y_step
    above, below = lax.rem(me + 4, size), lax.rem(me + size - 4, size)
    greet([{"row": d} for d in (x_near, y_near, above, below)] + col_peers(groups))
    others = []
    depth = turned.shape[0] // chunks

    def send(kind, chunk, source, slot, device):
        lines = pl.ds(chunk * depth, depth)
        copy = pltpu.make_async_remote_copy(
            src_ref=source.at[lines], dst_ref=panels.at[slot, lines],
            send_sem=send_sem.at[kind, chunk], recv_sem=recv_sem.at[kind, chunk],
            device_id={"row": device}, device_id_type=pl.DeviceIdType.MESH,
        )
        copy.start()
        others.append(copy)
        return copy

    def pass_on(kind, chunk):
        step = steps[kind]
        sign = jnp.where(step > 0, 1, -1)
        target = lax.rem(me + 4 * sign + size, size)
        late.append(send(3 + kind, chunk, panels.at[3 + step], 3 + step - 4 * sign, target))

    late, arriving = [], []
    for chunk in range(chunks):
        for pair in range(chunk * depth, (chunk + 1) * depth):
            turn(block, turned, pair)
        arriving.append((
            send(0, chunk, turned, 3 - x_step, x_near),
            send(1, chunk, turned, 3 - y_step, y_near),
        ))
    own = pltpu.make_async_copy(turned, panels.at[3], own_sem)
    own.start()
    col_copies = share_with_peers(groups, block, shared, col_send, col_recv)
    corner = []
    lag = 2
    for chunk in range(chunks + lag):
        if chunk < chunks:
            arriving[chunk][0].wait_recv()
            if chunk % 2 == 0:
                corner.append(send(2, chunk, panels.at[3 + x_step], 3 + x_step - y_step, y_near))
            pass_on(0, chunk)
            arriving[chunk][1].wait_recv()
            if chunk % 2 == 1:
                corner.append(send(2, chunk, panels.at[3 + y_step], 3 + y_step - x_step, x_near))
            pass_on(1, chunk)
        if chunk >= lag:
            corner[chunk - lag].wait_recv()
            pass_on(2, chunk - lag)
    for copy in late:
        copy.wait_recv()
    for copy in others:
        copy.wait_send()
    for copy in col_copies:
        copy.wait()
    own.wait()


def fetch(density, groups, size, span, planes):
    chunks = 8
    if planes:
        body, shape = functools.partial(relay_kernel, groups, size, chunks), (6, chunks)
    else:
        body, shape = functools.partial(direct_kernel, groups, size, span), (2 * span,)
    anywhere = pl.BlockSpec(memory_space=pl.ANY)
    rows, width, depth = density.shape
    turned = (rows // 2, depth, 2 * width)
    panels, shared = pl.pallas_call(
        body,
        in_specs=[pl.BlockSpec(memory_space=pltpu.VMEM)],
        out_specs=[anywhere, anywhere],
        out_shape=[
            jax.ShapeDtypeStruct((2 * span + 1,) + turned, density.dtype),
            jax.ShapeDtypeStruct((groups - 1,) + density.shape, density.dtype),
        ],
        scratch_shapes=[
            pltpu.VMEM(turned, density.dtype),
            pltpu.SemaphoreType.DMA,
            pltpu.SemaphoreType.DMA((groups - 1, PIECES)),
            pltpu.SemaphoreType.DMA((groups - 1, PIECES)),
            pltpu.SemaphoreType.DMA(shape),
            pltpu.SemaphoreType.DMA(shape),
        ],
        compiler_params=pltpu.CompilerParams(
            collective_id=0, has_side_effects=True, vmem_limit_bytes=32 * 1024 * 1024
        ),
    )(density)
    return panels.reshape((-1,) + turned[1:]), shared


def live_list(columns, rows, width, group_size, span):
    total, stored = columns.shape
    base = lax.axis_index("row") * rows
    first = lax.axis_index("col") * group_size
    own = lax.dynamic_slice_in_dim(columns, base, rows, 0)
    wanted = lax.dynamic_slice_in_dim(own, first, group_size, 1)
    group = lax.dynamic_slice_in_dim(columns, first, group_size, 1)
    candidates = jnp.take(group, own, axis=0)
    distance = jnp.mod(own - base + span * rows, total)
    equal = candidates[:, :, :, None] == wanted[:, None, None, :]
    slots = jnp.arange(group_size, dtype=jnp.int32)
    live = jnp.any(equal, axis=-1)
    place = jnp.sum(jnp.where(equal, slots, 0), axis=-1)
    inner = jnp.mod(jnp.arange(stored, dtype=jnp.int32) - first, stored)[None, :, None]
    code = ((distance[:, :, None] * group_size + slots) * stored + inner) * group_size + place
    flat = live.reshape(rows, stored * group_size)
    code = code.reshape(rows, stored * group_size)
    order = jnp.cumsum(flat.astype(jnp.int32), axis=1)
    ranks = jnp.arange(1, stored * group_size + 1, dtype=jnp.int32)
    chosen = flat[:, None, :] & (order[:, None, :] == ranks[None, :, None])
    packed = jnp.sum(jnp.where(chosen, code[:, None, :] + 1, 0), axis=-1)
    return order[:, -1], packed - 1


def multiply(right_ref, left_refs):
    depth = left_refs[0].shape[-1]
    total, start = None, 0
    for left_ref in left_refs:
        part = lax.dot_general(
            right_ref[0, :, start:start + depth], left_ref[...], (((1,), (1,)), ((), ())),
            preferred_element_type=jnp.float32,
        )
        total = part if total is None else total + part
        start += depth
    return total.T


def left_parts(own_ref, shared_ref):
    return [own_ref.at[0]] + [shared_ref.at[step, 0] for step in range(shared_ref.shape[0])]


def first_kernel(stored, group_size, width, count_ref, code_ref, panels_ref, own_ref, shared_ref, right_ref, square_ref):
    row = pl.program_id(0)
    right_ref[...] = jnp.zeros_like(right_ref)
    half = lax.broadcasted_iota(jnp.int32, (width, 2 * width), 1) >= width

    def one(entry, carry):
        pieces = []
        for part in range(UNROLL):
            raw = code_ref[row, entry * UNROLL + part]
            real = raw >= 0
            code = jnp.maximum(raw, 0)
            place = lax.rem(code, group_size)
            code = lax.div(code, group_size)
            inner = lax.rem(code, stored)
            code = lax.div(code, stored)
            slot = lax.rem(code, group_size)
            source = lax.div(code, group_size)
            value = panels_ref[lax.div(source, 2), pl.ds(pl.multiple_of(slot * width, width), width), :]
            swapped = jnp.concatenate([value[:, width:], value[:, :width]], axis=1)
            odd = lax.rem(inner, 2)
            same = jnp.full(value.shape, lax.rem(source, 2), jnp.int32) == odd
            value = jnp.where(same, value, swapped)
            mine = (half == (jnp.full(value.shape, odd, jnp.int32) == 1)) & jnp.full(value.shape, real)
            pieces.append((inner, place, jnp.where(mine, value, jnp.zeros_like(value))))
        for inner, place, value in pieces:
            lanes = pl.ds(pl.multiple_of(lax.div(inner, 2) * 2 * width, 2 * width), 2 * width)
            lines = pl.ds(pl.multiple_of(place * width, width), width)
            right_ref[0, lines, lanes] += value
        return carry

    lax.fori_loop(0, lax.div(count_ref[row] + UNROLL - 1, UNROLL), one, 0)
    square_ref[0] = multiply(right_ref, left_parts(own_ref, shared_ref)).astype(square_ref.dtype)


def second_kernel(own_ref, shared_ref, right_ref, out_ref):
    total = multiply(right_ref, left_parts(own_ref, shared_ref))
    out_ref[0] = 3.0 * own_ref[0].astype(jnp.float32) - 2.0 * total


def shards(density, columns):
    rows, width, depth = density.shape
    total, stored = columns.shape
    group_size = depth // width
    groups = stored // group_size
    span = -(-REACH // rows)
    count, codes = live_list(columns, rows, width, group_size, span)
    size = lax.axis_size("row")
    planes = (size, groups, span) == (16, 2, 3)
    panels, shared = fetch(density, groups, size, span, planes)
    row_spec = pl.BlockSpec((1, width, depth), lambda i, *_: (i, 0, 0))
    shared_spec = pl.BlockSpec((groups - 1, 1, width, depth), lambda i, *_: (0, i, 0, 0))
    right_spec = pl.BlockSpec((1, depth, stored * width), lambda i, *_: (i, 0, 0))
    right, square = pl.pallas_call(
        functools.partial(first_kernel, stored, group_size, width),
        grid_spec=pltpu.PrefetchScalarGridSpec(
            num_scalar_prefetch=2,
            grid=(rows,),
            in_specs=[pl.BlockSpec(panels.shape, lambda i, *_: (0, 0, 0)), row_spec, shared_spec],
            out_specs=[right_spec, row_spec],
        ),
        out_shape=[
            jax.ShapeDtypeStruct((rows, depth, stored * width), density.dtype),
            jax.ShapeDtypeStruct(density.shape, density.dtype),
        ],
        compiler_params=pltpu.CompilerParams(vmem_limit_bytes=40 * 1024 * 1024),
    )(count, codes, panels, density, shared)
    return pl.pallas_call(
        second_kernel,
        grid=(rows,),
        in_specs=[row_spec, shared_spec, right_spec],
        out_specs=row_spec,
        out_shape=jax.ShapeDtypeStruct(density.shape, jnp.float32),
        compiler_params=pltpu.CompilerParams(vmem_limit_bytes=40 * 1024 * 1024),
    )(square, exchange(square, groups, 1), right)


def solution(mesh):
    placed = (P("row", None, "col"), P())
    return jax.shard_map(
        shards, mesh=mesh, in_specs=placed, out_specs=P("row", None, "col"), check_vma=False
    )
```

```python
import functools

import jax
import jax.numpy as jnp
from jax import lax
from jax.experimental import pallas as pl
from jax.experimental.pallas import tpu as pltpu
from jax.sharding import PartitionSpec as P

REACH = 48
UNROLL = 4
PIECES = 8


def greet(devices):
    barrier = pltpu.get_barrier_semaphore()
    for device in devices:
        pl.semaphore_signal(barrier, inc=1, device_id=device, device_id_type=pl.DeviceIdType.MESH)
    pl.semaphore_wait(barrier, len(devices))


def col_peers(groups):
    return [{"col": lax.rem(lax.axis_index("col") + step, groups)} for step in range(1, groups)]


def share_with_peers(groups, block, shared, send_sem, recv_sem):
    copies = []
    chunks = send_sem.shape[1]
    depth = block.shape[0] // chunks
    for step, peer in enumerate(col_peers(groups)):
        for chunk in range(chunks):
            lines = pl.ds(chunk * depth, depth)
            copies.append(pltpu.make_async_remote_copy(
                src_ref=block.at[lines], dst_ref=shared.at[groups - 2 - step, lines],
                send_sem=send_sem.at[step, chunk], recv_sem=recv_sem.at[step, chunk],
                device_id=peer, device_id_type=pl.DeviceIdType.MESH,
            ))
            copies[-1].start()
    return copies


def exchange_kernel(groups, block, shared, send_sem, recv_sem):
    greet(col_peers(groups))
    for copy in share_with_peers(groups, block, shared, send_sem, recv_sem):
        copy.wait()


def exchange(block, groups, collective_id):
    return pl.pallas_call(
        functools.partial(exchange_kernel, groups),
        in_specs=[pl.BlockSpec(memory_space=pl.ANY)],
        out_specs=pl.BlockSpec(memory_space=pl.ANY),
        out_shape=jax.ShapeDtypeStruct((groups - 1,) + block.shape, block.dtype),
        scratch_shapes=[pltpu.SemaphoreType.DMA((groups - 1, PIECES))] * 2,
        compiler_params=pltpu.CompilerParams(collective_id=collective_id, has_side_effects=True),
    )(block)


def turn(block, turned, pair):
    wide = jnp.concatenate([block[2 * pair], block[2 * pair + 1]], axis=0)
    turned[pair] = wide.T


def direct_kernel(groups, size, span, block, panels, shared, turned, own_sem, col_send, col_recv, send_sem, recv_sem):
    me = lax.axis_index("row")
    offsets = [d for d in range(-span, span + 1) if d != 0]
    greet([{"row": lax.rem(me + d + size, size)} for d in offsets] + col_peers(groups))
    copies = share_with_peers(groups, block, shared, col_send, col_recv)
    for pair in range(turned.shape[0]):
        turn(block, turned, pair)
    own = pltpu.make_async_copy(turned, panels.at[span], own_sem)
    own.start()
    for step, d in enumerate(offsets):
        copies.append(pltpu.make_async_remote_copy(
            src_ref=turned, dst_ref=panels.at[span - d], send_sem=send_sem.at[step], recv_sem=recv_sem.at[step],
            device_id={"row": lax.rem(me + d + size, size)}, device_id_type=pl.DeviceIdType.MESH,
        ))
        copies[-1].start()
    for copy in copies:
        copy.wait()
    own.wait()


def relay_kernel(groups, size, chunks, block, panels, shared, turned, own_sem, col_send, col_recv, send_sem, recv_sem):
    me = lax.axis_index("row")
    x_step = 1 - 2 * lax.rem(me, 2)
    y_step = 2 - 4 * lax.rem(lax.div(me, 2), 2)
    steps = [x_step, y_step, x_step + y_step]
    x_near, y_near = me + x_step, me + y_step
    above, below = lax.rem(me + 4, size), lax.rem(me + size - 4, size)
    greet([{"row": d} for d in (x_near, y_near, above, below)] + col_peers(groups))
    others = []
    depth = turned.shape[0] // chunks

    def send(kind, chunk, source, slot, device):
        lines = pl.ds(chunk * depth, depth)
        copy = pltpu.make_async_remote_copy(
            src_ref=source.at[lines], dst_ref=panels.at[slot, lines],
            send_sem=send_sem.at[kind, chunk], recv_sem=recv_sem.at[kind, chunk],
            device_id={"row": device}, device_id_type=pl.DeviceIdType.MESH,
        )
        copy.start()
        others.append(copy)
        return copy

    def pass_on(kind, chunk):
        step = steps[kind]
        sign = jnp.where(step > 0, 1, -1)
        target = lax.rem(me + 4 * sign + size, size)
        late.append(send(3 + kind, chunk, panels.at[3 + step], 3 + step - 4 * sign, target))

    late, arriving = [], []
    for chunk in range(chunks):
        for pair in range(chunk * depth, (chunk + 1) * depth):
            turn(block, turned, pair)
        arriving.append((
            send(0, chunk, turned, 3 - x_step, x_near),
            send(1, chunk, turned, 3 - y_step, y_near),
        ))
    own = pltpu.make_async_copy(turned, panels.at[3], own_sem)
    own.start()
    col_copies = share_with_peers(groups, block, shared, col_send, col_recv)
    corner = []
    lag = 2
    for chunk in range(chunks + lag):
        if chunk < chunks:
            arriving[chunk][0].wait_recv()
            if chunk % 2 == 0:
                corner.append(send(2, chunk, panels.at[3 + x_step], 3 + x_step - y_step, y_near))
            pass_on(0, chunk)
            arriving[chunk][1].wait_recv()
            if chunk % 2 == 1:
                corner.append(send(2, chunk, panels.at[3 + y_step], 3 + y_step - x_step, x_near))
            pass_on(1, chunk)
        if chunk >= lag:
            corner[chunk - lag].wait_recv()
            pass_on(2, chunk - lag)
    for copy in late:
        copy.wait_recv()
    for copy in others:
        copy.wait_send()
    for copy in col_copies:
        copy.wait()
    own.wait()


def fetch(density, groups, size, span, planes):
    chunks = 8
    if planes:
        body, shape = functools.partial(relay_kernel, groups, size, chunks), (6, chunks)
    else:
        body, shape = functools.partial(direct_kernel, groups, size, span), (2 * span,)
    anywhere = pl.BlockSpec(memory_space=pl.ANY)
    rows, width, depth = density.shape
    turned = (rows // 2, depth, 2 * width)
    panels, shared = pl.pallas_call(
        body,
        in_specs=[pl.BlockSpec(memory_space=pltpu.VMEM)],
        out_specs=[anywhere, anywhere],
        out_shape=[
            jax.ShapeDtypeStruct((2 * span + 1,) + turned, density.dtype),
            jax.ShapeDtypeStruct((groups - 1,) + density.shape, density.dtype),
        ],
        scratch_shapes=[
            pltpu.VMEM(turned, density.dtype),
            pltpu.SemaphoreType.DMA,
            pltpu.SemaphoreType.DMA((groups - 1, PIECES)),
            pltpu.SemaphoreType.DMA((groups - 1, PIECES)),
            pltpu.SemaphoreType.DMA(shape),
            pltpu.SemaphoreType.DMA(shape),
        ],
        compiler_params=pltpu.CompilerParams(
            collective_id=0, has_side_effects=True, vmem_limit_bytes=32 * 1024 * 1024
        ),
    )(density)
    return panels.reshape((-1,) + turned[1:]), shared


def live_list(columns, rows, width, group_size, span):
    total, stored = columns.shape
    base = lax.axis_index("row") * rows
    first = lax.axis_index("col") * group_size
    own = lax.dynamic_slice_in_dim(columns, base, rows, 0)
    wanted = lax.dynamic_slice_in_dim(own, first, group_size, 1)
    group = lax.dynamic_slice_in_dim(columns, first, group_size, 1)
    candidates = jnp.take(group, own, axis=0)
    distance = jnp.mod(own - base + span * rows, total)
    equal = candidates[:, :, :, None] == wanted[:, None, None, :]
    slots = jnp.arange(group_size, dtype=jnp.int32)
    live = jnp.any(equal, axis=-1)
    place = jnp.sum(jnp.where(equal, slots, 0), axis=-1)
    inner = jnp.mod(jnp.arange(stored, dtype=jnp.int32) - first, stored)[None, :, None]
    code = ((distance[:, :, None] * group_size + slots) * stored + inner) * group_size + place
    flat = live.reshape(rows, stored * group_size)
    code = code.reshape(rows, stored * group_size)
    order = jnp.cumsum(flat.astype(jnp.int32), axis=1)
    ranks = jnp.arange(1, stored * group_size + 1, dtype=jnp.int32)
    chosen = flat[:, None, :] & (order[:, None, :] == ranks[None, :, None])
    packed = jnp.sum(jnp.where(chosen, code[:, None, :] + 1, 0), axis=-1)
    return order[:, -1], packed - 1


def multiply(right, left_refs):
    depth = left_refs[0].shape[-1]
    total, start = None, 0
    for left_ref in left_refs:
        part = lax.dot_general(
            right[:, start:start + depth], left_ref[...], (((1,), (1,)), ((), ())),
            preferred_element_type=jnp.float32,
        )
        total = part if total is None else total + part
        start += depth
    return total.T


def left_parts(own_ref, shared_ref, row):
    return [own_ref.at[row]] + [shared_ref.at[step, row] for step in range(shared_ref.shape[0])]


def first_kernel(stored, group_size, width, count_ref, code_ref, panels_ref, own_ref, shared_ref, right_hbm, square_ref, rights, leave_sem):
    row = pl.program_id(0)
    rows, depth, _ = rights.shape
    right_ref = rights.at[row]
    right_ref[...] = jnp.zeros(right_ref.shape, right_ref.dtype)
    half = lax.broadcasted_iota(jnp.int32, (width, 2 * width), 1) >= width

    def one(entry, carry):
        pieces = []
        for part in range(UNROLL):
            raw = code_ref[row, entry * UNROLL + part]
            real = raw >= 0
            code = jnp.maximum(raw, 0)
            place = lax.rem(code, group_size)
            code = lax.div(code, group_size)
            inner = lax.rem(code, stored)
            code = lax.div(code, stored)
            slot = lax.rem(code, group_size)
            source = lax.div(code, group_size)
            value = panels_ref[lax.div(source, 2), pl.ds(pl.multiple_of(slot * width, width), width), :]
            swapped = jnp.concatenate([value[:, width:], value[:, :width]], axis=1)
            odd = lax.rem(inner, 2)
            same = jnp.full(value.shape, lax.rem(source, 2), jnp.int32) == odd
            value = jnp.where(same, value, swapped)
            mine = (half == (jnp.full(value.shape, odd, jnp.int32) == 1)) & jnp.full(value.shape, real)
            pieces.append((inner, place, jnp.where(mine, value, jnp.zeros_like(value))))
        for inner, place, value in pieces:
            lanes = pl.ds(pl.multiple_of(lax.div(inner, 2) * 2 * width, 2 * width), 2 * width)
            lines = pl.ds(pl.multiple_of(place * width, width), width)
            right_ref[lines, lanes] += value
        return carry

    lax.fori_loop(0, lax.div(count_ref[row] + UNROLL - 1, UNROLL), one, 0)
    wide = 2 * width

    def leave(which, part):
        lines = pl.ds(part * wide, wide)
        return pltpu.make_async_copy(
            rights.at[which, lines], right_hbm.at[which, lines], leave_sem.at[which, part]
        )

    for part in range(depth // wide):
        leave(row, part).start()
    total = multiply(right_ref[...], left_parts(own_ref, shared_ref, 0))
    square_ref[0] = total.astype(square_ref.dtype)

    @pl.when(row == rows - 1)
    def _():
        for which in range(rows):
            for part in range(depth // wide):
                leave(which, part).wait()


def second_kernel(own_ref, shared_ref, *refs):
    *right_refs, out_ref = refs
    wide = right_refs[0].shape[1]
    for row in range(own_ref.shape[0]):
        for part, right_ref in enumerate(right_refs):
            lanes = slice(part * wide, (part + 1) * wide)
            total = multiply(right_ref[row], left_parts(own_ref, shared_ref, row))
            out_ref[row, :, lanes] = 3.0 * own_ref[row, :, lanes].astype(jnp.float32) - 2.0 * total


def shards(density, columns):
    rows, width, depth = density.shape
    total, stored = columns.shape
    group_size = depth // width
    groups = stored // group_size
    span = -(-REACH // rows)
    count, codes = live_list(columns, rows, width, group_size, span)
    size = lax.axis_size("row")
    planes = (size, groups, span) == (16, 2, 3)
    panels, shared = fetch(density, groups, size, span, planes)
    row_spec = pl.BlockSpec((1, width, depth), lambda i, *_: (i, 0, 0))
    shared_spec = pl.BlockSpec((groups - 1, 1, width, depth), lambda i, *_: (0, i, 0, 0))
    parts = depth // (2 * width)
    right, square = pl.pallas_call(
        functools.partial(first_kernel, stored, group_size, width),
        grid_spec=pltpu.PrefetchScalarGridSpec(
            num_scalar_prefetch=2,
            grid=(rows,),
            in_specs=[pl.BlockSpec(panels.shape, lambda i, *_: (0, 0, 0)), row_spec, shared_spec],
            out_specs=[pl.BlockSpec(memory_space=pl.ANY), row_spec],
            scratch_shapes=[
                pltpu.VMEM((rows, depth, stored * width), density.dtype),
                pltpu.SemaphoreType.DMA((rows, parts)),
            ],
        ),
        out_shape=[
            jax.ShapeDtypeStruct((rows, depth, stored * width), density.dtype),
            jax.ShapeDtypeStruct(density.shape, density.dtype),
        ],
        compiler_params=pltpu.CompilerParams(vmem_limit_bytes=40 * 1024 * 1024),
    )(count, codes, panels, density, shared)
    two_spec = pl.BlockSpec((2, width, depth), lambda i: (i, 0, 0))
    shared_two = pl.BlockSpec((groups - 1, 2, width, depth), lambda i: (0, i, 0, 0))
    part_specs = [
        pl.BlockSpec((2, 2 * width, stored * width), functools.partial(lambda part, i: (i, part, 0), part))
        for part in range(parts)
    ]
    return pl.pallas_call(
        second_kernel,
        grid=(rows // 2,),
        in_specs=[two_spec, shared_two] + part_specs,
        out_specs=two_spec,
        out_shape=jax.ShapeDtypeStruct(density.shape, jnp.float32),
        compiler_params=pltpu.CompilerParams(vmem_limit_bytes=40 * 1024 * 1024),
    )(square, exchange(square, groups, 1), *([right] * parts))


def solution(mesh):
    placed = (P("row", None, "col"), P())
    return jax.shard_map(
        shards, mesh=mesh, in_specs=placed, out_specs=P("row", None, "col"), check_vma=False
    )
```

```python
import functools

import jax
import jax.numpy as jnp
import numpy as np
from jax import lax
from jax.experimental import pallas as pl
from jax.experimental.pallas import tpu as pltpu
from jax.sharding import PartitionSpec as P

REACH = 48
UNROLL = 4
PIECES = 8


def greet(devices):
    barrier = pltpu.get_barrier_semaphore()
    for device in devices:
        pl.semaphore_signal(barrier, inc=1, device_id=device, device_id_type=pl.DeviceIdType.MESH)
    pl.semaphore_wait(barrier, len(devices))


def col_peers(groups):
    return [{"col": lax.rem(lax.axis_index("col") + step, groups)} for step in range(1, groups)]


def share_with_peers(groups, block, shared, send_sem, recv_sem):
    copies = []
    chunks = send_sem.shape[1]
    depth = block.shape[0] // chunks
    for step, peer in enumerate(col_peers(groups)):
        for chunk in range(chunks):
            lines = pl.ds(chunk * depth, depth)
            copies.append(pltpu.make_async_remote_copy(
                src_ref=block.at[lines], dst_ref=shared.at[groups - 2 - step, lines],
                send_sem=send_sem.at[step, chunk], recv_sem=recv_sem.at[step, chunk],
                device_id=peer, device_id_type=pl.DeviceIdType.MESH,
            ))
            copies[-1].start()
    return copies


def exchange_kernel(groups, block, shared, send_sem, recv_sem):
    greet(col_peers(groups))
    for copy in share_with_peers(groups, block, shared, send_sem, recv_sem):
        copy.wait()


def exchange(block, groups, collective_id):
    return pl.pallas_call(
        functools.partial(exchange_kernel, groups),
        in_specs=[pl.BlockSpec(memory_space=pl.ANY)],
        out_specs=pl.BlockSpec(memory_space=pl.ANY),
        out_shape=jax.ShapeDtypeStruct((groups - 1,) + block.shape, block.dtype),
        scratch_shapes=[pltpu.SemaphoreType.DMA((groups - 1, PIECES))] * 2,
        compiler_params=pltpu.CompilerParams(collective_id=collective_id, has_side_effects=True),
    )(block)


def turn(block, turned, pair):
    wide = jnp.concatenate([block[2 * pair], block[2 * pair + 1]], axis=0)
    turned[pair] = wide.T


def direct_kernel(groups, size, span, block, panels, shared, turned, own_sem, col_send, col_recv, send_sem, recv_sem):
    me = lax.axis_index("row")
    offsets = [d for d in range(-span, span + 1) if d != 0]
    greet([{"row": lax.rem(me + d + size, size)} for d in offsets] + col_peers(groups))
    copies = share_with_peers(groups, block, shared, col_send, col_recv)
    for pair in range(turned.shape[0]):
        turn(block, turned, pair)
    own = pltpu.make_async_copy(turned, panels.at[span], own_sem)
    own.start()
    for step, d in enumerate(offsets):
        copies.append(pltpu.make_async_remote_copy(
            src_ref=turned, dst_ref=panels.at[span - d], send_sem=send_sem.at[step], recv_sem=recv_sem.at[step],
            device_id={"row": lax.rem(me + d + size, size)}, device_id_type=pl.DeviceIdType.MESH,
        ))
        copies[-1].start()
    for copy in copies:
        copy.wait()
    own.wait()


def relay_kernel(groups, size, chunks, block, panels, shared, turned, own_sem, col_send, col_recv, send_sem, recv_sem, held, up_send, up_recv):
    me = lax.axis_index("row")
    x_step = 1 - 2 * lax.rem(me, 2)
    y_step = 2 - 4 * lax.rem(lax.div(me, 2), 2)
    steps = [x_step, y_step, x_step + y_step]
    x_near, y_near = me + x_step, me + y_step
    above, below = lax.rem(me + 4, size), lax.rem(me + size - 4, size)
    greet([{"row": d} for d in (x_near, y_near, above, below)] + col_peers(groups))
    others = []
    depth = turned.shape[0] // chunks

    def send(kind, chunk, source, slot, device):
        lines = pl.ds(chunk * depth, depth)
        copy = pltpu.make_async_remote_copy(
            src_ref=source.at[lines], dst_ref=panels.at[slot, lines],
            send_sem=send_sem.at[kind, chunk], recv_sem=recv_sem.at[kind, chunk],
            device_id={"row": device}, device_id_type=pl.DeviceIdType.MESH,
        )
        copy.start()
        others.append(copy)
        return copy

    def from_held(kind, chunk, way, slot, device):
        lines = pl.ds(chunk * depth, depth)
        copy = pltpu.make_async_remote_copy(
            src_ref=held.at[way, chunk // 2], dst_ref=panels.at[slot, lines],
            send_sem=send_sem.at[kind, chunk], recv_sem=recv_sem.at[kind, chunk],
            device_id={"row": device}, device_id_type=pl.DeviceIdType.MESH,
        )
        copy.start()
        others.append(copy)
        return copy

    def pass_on(kind, chunk):
        step = steps[kind]
        sign = jnp.where(step > 0, 1, -1)
        target = lax.rem(me + 4 * sign + size, size)
        late.append(send(3 + kind, chunk, panels.at[3 + step], 3 + step - 4 * sign, target))

    place = lax.rem(me, 4)
    x_sign, y_sign = x_step, lax.div(y_step, 2)
    x_held = lax.div(1 + x_sign, 2)
    y_held = lax.div(1 + y_sign, 2)

    def level(way, chunk):
        lines = pl.ds(chunk * depth, depth)
        return pltpu.make_async_remote_copy(
            src_ref=turned.at[lines], dst_ref=held.at[way, chunk // 2],
            send_sem=up_send.at[way, chunk // 2], recv_sem=up_recv.at[way, chunk // 2],
            device_id={"row": above if way == 0 else below}, device_id_type=pl.DeviceIdType.MESH,
        )

    def on_level(chunk, act):
        @pl.when(place > 0)
        def _():
            act(level(0, chunk))

        @pl.when(place < 3)
        def _():
            act(level(1, chunk))

    late, arriving = [], []
    for chunk in range(chunks):
        for pair in range(chunk * depth, (chunk + 1) * depth):
            turn(block, turned, pair)
        if chunk % 2 == 0:
            on_level(chunk, lambda copy: copy.start())
        arriving.append((
            send(0, chunk, turned, 3 - x_step, x_near),
            send(1, chunk, turned, 3 - y_step, y_near),
        ))
    own = pltpu.make_async_copy(turned, panels.at[3], own_sem)
    own.start()
    col_copies = share_with_peers(groups, block, shared, col_send, col_recv)
    corner, spread = {}, {}
    lag = 2
    for chunk in range(chunks + lag):
        if chunk < chunks:
            by_y = chunk % 4 != 1
            arriving[chunk][0].wait_recv()
            if by_y:
                corner[chunk] = send(2, chunk, panels.at[3 + x_step], 3 + x_step - y_step, y_near)
            if chunk % 2 == 1:
                pass_on(0, chunk)
            arriving[chunk][1].wait_recv()
            if not by_y:
                corner[chunk] = send(2, chunk, panels.at[3 + y_step], 3 + y_step - x_step, x_near)
            if chunk % 2 == 1:
                pass_on(1, chunk)
            else:
                on_level(chunk, lambda copy: copy.wait_recv())
                late.append(from_held(3, chunk, x_held, 3 - x_step + 4 * x_sign, x_near))
                spread[chunk] = from_held(4, chunk, y_held, 3 - y_step + 4 * y_sign, y_near)
        done = chunk - lag
        if done >= 0:
            corner[done].wait_recv()
            if done % 2 == 1:
                pass_on(2, done)
            else:
                spread[done].wait_recv()
                slot = 3 + y_step - 4 * y_sign
                late.append(send(5, done, panels.at[slot], slot - x_step, x_near))
    for copy in late:
        copy.wait_recv()
    for chunk in range(0, chunks, 2):
        on_level(chunk, lambda copy: copy.wait_send())
    for copy in others:
        copy.wait_send()
    for copy in col_copies:
        copy.wait()
    own.wait()


def fetch(density, groups, size, span, planes):
    chunks = 8
    if planes:
        body, shape = functools.partial(relay_kernel, groups, size, chunks), (6, chunks)
    else:
        body, shape = functools.partial(direct_kernel, groups, size, span), (2 * span,)
    anywhere = pl.BlockSpec(memory_space=pl.ANY)
    rows, width, depth = density.shape
    turned = (rows // 2, depth, 2 * width)
    extra = []
    if planes:
        extra = [
            pltpu.VMEM((2, chunks // 2, rows // 2 // chunks, depth, 2 * width), density.dtype),
            pltpu.SemaphoreType.DMA((2, chunks // 2)),
            pltpu.SemaphoreType.DMA((2, chunks // 2)),
        ]
    panels, shared = pl.pallas_call(
        body,
        in_specs=[pl.BlockSpec(memory_space=pltpu.VMEM)],
        out_specs=[anywhere, anywhere],
        out_shape=[
            jax.ShapeDtypeStruct((2 * span + 1,) + turned, density.dtype),
            jax.ShapeDtypeStruct((groups - 1,) + density.shape, density.dtype),
        ],
        scratch_shapes=[
            pltpu.VMEM(turned, density.dtype),
            pltpu.SemaphoreType.DMA,
            pltpu.SemaphoreType.DMA((groups - 1, PIECES)),
            pltpu.SemaphoreType.DMA((groups - 1, PIECES)),
            pltpu.SemaphoreType.DMA(shape),
            pltpu.SemaphoreType.DMA(shape),
        ] + extra,
        compiler_params=pltpu.CompilerParams(
            collective_id=0, has_side_effects=True, vmem_limit_bytes=32 * 1024 * 1024
        ),
    )(density)
    return panels.reshape((-1,) + turned[1:]), shared


def live_list(columns, rows, width, group_size, span):
    total, stored = columns.shape
    base = lax.axis_index("row") * rows
    first = lax.axis_index("col") * group_size
    own = lax.dynamic_slice_in_dim(columns, base, rows, 0)
    wanted = lax.dynamic_slice_in_dim(own, first, group_size, 1)
    group = lax.dynamic_slice_in_dim(columns, first, group_size, 1)
    candidates = jnp.take(group, own, axis=0)
    distance = jnp.mod(own - base + span * rows, total)
    equal = candidates[:, :, :, None] == wanted[:, None, None, :]
    slots = jnp.arange(group_size, dtype=jnp.int32)
    live = jnp.any(equal, axis=-1)
    place = jnp.sum(jnp.where(equal, slots, 0), axis=-1)
    inner = jnp.mod(jnp.arange(stored, dtype=jnp.int32) - first, stored)[None, :, None]
    odd = jnp.mod(inner, 2)
    flip = (jnp.mod(distance[:, :, None], 2) != odd).astype(jnp.int32)
    code = (distance[:, :, None] // 2) * 256 + slots
    code = (code * 256 + inner // 2) * 16 + place
    code = code * 4 + flip * 2 + odd
    flat = live.reshape(rows, stored * group_size)
    code = code.reshape(rows, stored * group_size)
    order = jnp.cumsum(flat.astype(jnp.int32), axis=1)
    ranks = jnp.arange(1, stored * group_size + 1, dtype=jnp.int32)
    chosen = flat[:, None, :] & (order[:, None, :] == ranks[None, :, None])
    packed = jnp.sum(jnp.where(chosen, code[:, None, :] + 1, 0), axis=-1)
    return order[:, -1], packed - 1


def half_factors(width, dtype):
    high = np.arange(2 * width) >= width
    factors = np.zeros((5, 2, width, 2 * width), np.float32)
    for flip in range(2):
        for odd in range(2):
            factors[2 * flip + odd, flip] = high == bool(odd)
    return jnp.asarray(factors, dtype)


def multiply(right, left_refs):
    depth = left_refs[0].shape[-1]
    total, start = None, 0
    for left_ref in left_refs:
        part = lax.dot_general(
            right[:, start:start + depth], left_ref[...], (((1,), (1,)), ((), ())),
            preferred_element_type=jnp.float32,
        )
        total = part if total is None else total + part
        start += depth
    return total.T


def left_parts(own_ref, shared_ref, row):
    return [own_ref.at[row]] + [shared_ref.at[step, row] for step in range(shared_ref.shape[0])]


def first_kernel(stored, group_size, width, count_ref, code_ref, panels_ref, halves_ref, own_ref, shared_ref, right_hbm, square_ref, rights, leave_sem):
    row = pl.program_id(0)
    rows, depth, _ = rights.shape
    right_ref = rights.at[row]
    right_ref[...] = jnp.zeros(right_ref.shape, right_ref.dtype)

    def one(entry, carry):
        pieces = []
        for part in range(UNROLL):
            raw = code_ref[row, entry * UNROLL + part]
            kind = jnp.where(raw >= 0, raw & 3, 4)
            code = jnp.maximum(raw, 0)
            place, inner = (code >> 2) & 15, (code >> 6) & 255
            slot, source = (code >> 14) & 255, code >> 22
            value = panels_ref[source, pl.ds(pl.multiple_of(slot * width, width), width), :]
            swapped = jnp.concatenate([value[:, width:], value[:, :width]], axis=1)
            keep, turn_over = halves_ref[kind, 0], halves_ref[kind, 1]
            pieces.append((inner, place, value * keep + swapped * turn_over))
        for inner, place, value in pieces:
            lanes = pl.ds(pl.multiple_of(inner * 2 * width, 2 * width), 2 * width)
            lines = pl.ds(pl.multiple_of(place * width, width), width)
            right_ref[lines, lanes] += value
        return carry

    lax.fori_loop(0, lax.div(count_ref[row] + UNROLL - 1, UNROLL), one, 0)
    wide = 2 * width

    def leave(which, part):
        lines = pl.ds(part * wide, wide)
        return pltpu.make_async_copy(
            rights.at[which, lines], right_hbm.at[which, lines], leave_sem.at[which, part]
        )

    for part in range(depth // wide):
        leave(row, part).start()
    total = multiply(right_ref[...], left_parts(own_ref, shared_ref, 0))
    square_ref[0] = total.astype(square_ref.dtype)

    @pl.when(row == rows - 1)
    def _():
        for which in range(rows):
            for part in range(depth // wide):
                leave(which, part).wait()


def second_kernel(own_ref, shared_ref, *refs):
    *right_refs, out_ref = refs
    wide = right_refs[0].shape[1]
    for row in range(own_ref.shape[0]):
        for part, right_ref in enumerate(right_refs):
            lanes = slice(part * wide, (part + 1) * wide)
            total = multiply(right_ref[row], left_parts(own_ref, shared_ref, row))
            out_ref[row, :, lanes] = 3.0 * own_ref[row, :, lanes].astype(jnp.float32) - 2.0 * total


def shards(density, columns):
    rows, width, depth = density.shape
    total, stored = columns.shape
    group_size = depth // width
    groups = stored // group_size
    span = -(-REACH // rows)
    count, codes = live_list(columns, rows, width, group_size, span)
    size = lax.axis_size("row")
    planes = (size, groups, span) == (16, 2, 3)
    panels, shared = fetch(density, groups, size, span, planes)
    halves = half_factors(width, density.dtype)
    row_spec = pl.BlockSpec((1, width, depth), lambda i, *_: (i, 0, 0))
    shared_spec = pl.BlockSpec((groups - 1, 1, width, depth), lambda i, *_: (0, i, 0, 0))
    parts = depth // (2 * width)
    right, square = pl.pallas_call(
        functools.partial(first_kernel, stored, group_size, width),
        grid_spec=pltpu.PrefetchScalarGridSpec(
            num_scalar_prefetch=2,
            grid=(rows,),
            in_specs=[
                pl.BlockSpec(panels.shape, lambda i, *_: (0, 0, 0)),
                pl.BlockSpec(halves.shape, lambda i, *_: (0, 0, 0, 0)),
                row_spec, shared_spec,
            ],
            out_specs=[pl.BlockSpec(memory_space=pl.ANY), row_spec],
            scratch_shapes=[
                pltpu.VMEM((rows, depth, stored * width), density.dtype),
                pltpu.SemaphoreType.DMA((rows, parts)),
            ],
        ),
        out_shape=[
            jax.ShapeDtypeStruct((rows, depth, stored * width), density.dtype),
            jax.ShapeDtypeStruct(density.shape, density.dtype),
        ],
        compiler_params=pltpu.CompilerParams(vmem_limit_bytes=40 * 1024 * 1024),
    )(count, codes, panels, halves, density, shared)
    two_spec = pl.BlockSpec((2, width, depth), lambda i: (i, 0, 0))
    shared_two = pl.BlockSpec((groups - 1, 2, width, depth), lambda i: (0, i, 0, 0))
    part_specs = [
        pl.BlockSpec((2, 2 * width, stored * width), functools.partial(lambda part, i: (i, part, 0), part))
        for part in range(parts)
    ]
    return pl.pallas_call(
        second_kernel,
        grid=(rows // 2,),
        in_specs=[two_spec, shared_two] + part_specs,
        out_specs=two_spec,
        out_shape=jax.ShapeDtypeStruct(density.shape, jnp.float32),
        compiler_params=pltpu.CompilerParams(vmem_limit_bytes=40 * 1024 * 1024),
    )(square, exchange(square, groups, 1), *([right] * parts))


def solution(mesh):
    placed = (P("row", None, "col"), P())
    return jax.shard_map(
        shards, mesh=mesh, in_specs=placed, out_specs=P("row", None, "col"), check_vma=False
    )
```

```python
import functools

import jax
import jax.numpy as jnp
from jax import lax
from jax.experimental import pallas as pl
from jax.experimental.pallas import tpu as pltpu
from jax.sharding import PartitionSpec as P

REACH = 48
UNROLL = 4
PIECES = 8
LIMIT = 8 * 1024 * 1024


def greet(devices):
    barrier = pltpu.get_barrier_semaphore()
    for device in devices:
        pl.semaphore_signal(barrier, inc=1, device_id=device, device_id_type=pl.DeviceIdType.MESH)
    pl.semaphore_wait(barrier, len(devices))


def col_peers(groups):
    return [{"col": lax.rem(lax.axis_index("col") + step, groups)} for step in range(1, groups)]


def share_with_peers(groups, block, shared, first, send_sem, recv_sem):
    copies = []
    chunks = send_sem.shape[1]
    depth = block.shape[0] // chunks
    for step, peer in enumerate(col_peers(groups)):
        for chunk in range(chunks):
            lines = pl.ds(chunk * depth, depth)
            copies.append(pltpu.make_async_remote_copy(
                src_ref=block.at[lines], dst_ref=shared.at[first + groups - 2 - step, lines],
                send_sem=send_sem.at[step, chunk], recv_sem=recv_sem.at[step, chunk],
                device_id=peer, device_id_type=pl.DeviceIdType.MESH,
            ))
            copies[-1].start()
    return copies


def exchange_kernel(groups, block, shared, send_sem, recv_sem):
    greet(col_peers(groups))
    for copy in share_with_peers(groups, block, shared, 0, send_sem, recv_sem):
        copy.wait()


def exchange(block, groups, collective_id):
    return pl.pallas_call(
        functools.partial(exchange_kernel, groups),
        in_specs=[pl.BlockSpec(memory_space=pltpu.VMEM)],
        out_specs=pl.BlockSpec(memory_space=pltpu.VMEM),
        out_shape=jax.ShapeDtypeStruct((groups - 1,) + block.shape, block.dtype),
        scratch_shapes=[pltpu.SemaphoreType.DMA((groups - 1, PIECES))] * 2,
        compiler_params=pltpu.CompilerParams(
            collective_id=collective_id, has_side_effects=True, vmem_limit_bytes=LIMIT
        ),
    )(block)


def turn(block, turned, pair):
    wide = jnp.concatenate([block[2 * pair], block[2 * pair + 1]], axis=0)
    turned[pair] = wide.T


def direct_kernel(groups, size, span, block, panels, shared, turned, own_sem, col_send, col_recv, send_sem, recv_sem):
    me = lax.axis_index("row")
    offsets = [d for d in range(-span, span + 1) if d != 0]
    greet([{"row": lax.rem(me + d + size, size)} for d in offsets] + col_peers(groups))
    copies = share_with_peers(groups, block, shared, 1, col_send, col_recv)
    shared[0] = block[...]
    for pair in range(turned.shape[0]):
        turn(block, turned, pair)
    own = pltpu.make_async_copy(turned, panels.at[span], own_sem)
    own.start()
    for step, d in enumerate(offsets):
        copies.append(pltpu.make_async_remote_copy(
            src_ref=turned, dst_ref=panels.at[span - d], send_sem=send_sem.at[step], recv_sem=recv_sem.at[step],
            device_id={"row": lax.rem(me + d + size, size)}, device_id_type=pl.DeviceIdType.MESH,
        ))
        copies[-1].start()
    for copy in copies:
        copy.wait()
    own.wait()


def relay_kernel(groups, size, chunks, block, panels, shared, turned, own_sem, col_send, col_recv, send_sem, recv_sem, held, up_send, up_recv):
    me = lax.axis_index("row")
    x_step = 1 - 2 * lax.rem(me, 2)
    y_step = 2 - 4 * lax.rem(lax.div(me, 2), 2)
    steps = [x_step, y_step, x_step + y_step]
    x_near, y_near = me + x_step, me + y_step
    above, below = lax.rem(me + 4, size), lax.rem(me + size - 4, size)
    greet([{"row": d} for d in (x_near, y_near, above, below)] + col_peers(groups))
    others = []
    depth = turned.shape[0] // chunks

    def send(kind, chunk, source, slot, device):
        lines = pl.ds(chunk * depth, depth)
        copy = pltpu.make_async_remote_copy(
            src_ref=source.at[lines], dst_ref=panels.at[slot, lines],
            send_sem=send_sem.at[kind, chunk], recv_sem=recv_sem.at[kind, chunk],
            device_id={"row": device}, device_id_type=pl.DeviceIdType.MESH,
        )
        copy.start()
        others.append(copy)
        return copy

    def from_held(kind, chunk, way, slot, device):
        lines = pl.ds(chunk * depth, depth)
        copy = pltpu.make_async_remote_copy(
            src_ref=held.at[way, chunk // 2], dst_ref=panels.at[slot, lines],
            send_sem=send_sem.at[kind, chunk], recv_sem=recv_sem.at[kind, chunk],
            device_id={"row": device}, device_id_type=pl.DeviceIdType.MESH,
        )
        copy.start()
        others.append(copy)
        return copy

    def pass_on(kind, chunk):
        step = steps[kind]
        sign = jnp.where(step > 0, 1, -1)
        target = lax.rem(me + 4 * sign + size, size)
        late.append(send(3 + kind, chunk, panels.at[3 + step], 3 + step - 4 * sign, target))

    place = lax.rem(me, 4)
    x_sign, y_sign = x_step, lax.div(y_step, 2)
    x_held = lax.div(1 + x_sign, 2)
    y_held = lax.div(1 + y_sign, 2)

    def level(way, chunk):
        lines = pl.ds(chunk * depth, depth)
        return pltpu.make_async_remote_copy(
            src_ref=turned.at[lines], dst_ref=held.at[way, chunk // 2],
            send_sem=up_send.at[way, chunk // 2], recv_sem=up_recv.at[way, chunk // 2],
            device_id={"row": above if way == 0 else below}, device_id_type=pl.DeviceIdType.MESH,
        )

    def on_level(chunk, act):
        @pl.when(place > 0)
        def _():
            act(level(0, chunk))

        @pl.when(place < 3)
        def _():
            act(level(1, chunk))

    late, arriving = [], []
    for chunk in range(chunks):
        for pair in range(chunk * depth, (chunk + 1) * depth):
            turn(block, turned, pair)
        if chunk % 2 == 0:
            on_level(chunk, lambda copy: copy.start())
        arriving.append((
            send(0, chunk, turned, 3 - x_step, x_near),
            send(1, chunk, turned, 3 - y_step, y_near),
        ))
    own = pltpu.make_async_copy(turned, panels.at[3], own_sem)
    own.start()
    col_copies = share_with_peers(groups, block, shared, 1, col_send, col_recv)
    shared[0] = block[...]
    corner, spread = {}, {}
    lag = 2
    for chunk in range(chunks + lag):
        if chunk < chunks:
            by_y = chunk % 4 != 1
            arriving[chunk][0].wait_recv()
            if by_y:
                corner[chunk] = send(2, chunk, panels.at[3 + x_step], 3 + x_step - y_step, y_near)
            if chunk % 2 == 1:
                pass_on(0, chunk)
            arriving[chunk][1].wait_recv()
            if not by_y:
                corner[chunk] = send(2, chunk, panels.at[3 + y_step], 3 + y_step - x_step, x_near)
            if chunk % 2 == 1:
                pass_on(1, chunk)
            else:
                on_level(chunk, lambda copy: copy.wait_recv())
                late.append(from_held(3, chunk, x_held, 3 - x_step + 4 * x_sign, x_near))
                spread[chunk] = from_held(4, chunk, y_held, 3 - y_step + 4 * y_sign, y_near)
        done = chunk - lag
        if done >= 0:
            corner[done].wait_recv()
            if done % 2 == 1:
                pass_on(2, done)
            else:
                spread[done].wait_recv()
                slot = 3 + y_step - 4 * y_sign
                late.append(send(5, done, panels.at[slot], slot - x_step, x_near))
    for copy in late:
        copy.wait_recv()
    for chunk in range(0, chunks, 2):
        on_level(chunk, lambda copy: copy.wait_send())
    for copy in others:
        copy.wait_send()
    for copy in col_copies:
        copy.wait()
    own.wait()


def fetch(density, groups, size, span, planes):
    chunks = 8
    if planes:
        body, shape = functools.partial(relay_kernel, groups, size, chunks), (6, chunks)
    else:
        body, shape = functools.partial(direct_kernel, groups, size, span), (2 * span,)
    inside = pl.BlockSpec(memory_space=pltpu.VMEM)
    rows, width, depth = density.shape
    turned = (rows // 2, depth, 2 * width)
    extra = []
    if planes:
        extra = [
            pltpu.VMEM((2, chunks // 2, rows // 2 // chunks, depth, 2 * width), density.dtype),
            pltpu.SemaphoreType.DMA((2, chunks // 2)),
            pltpu.SemaphoreType.DMA((2, chunks // 2)),
        ]
    panels, shared = pl.pallas_call(
        body,
        in_specs=[inside],
        out_specs=[inside, inside],
        out_shape=[
            jax.ShapeDtypeStruct((2 * span + 1,) + turned, density.dtype),
            jax.ShapeDtypeStruct((groups,) + density.shape, density.dtype),
        ],
        scratch_shapes=[
            pltpu.VMEM(turned, density.dtype),
            pltpu.SemaphoreType.DMA,
            pltpu.SemaphoreType.DMA((groups - 1, PIECES)),
            pltpu.SemaphoreType.DMA((groups - 1, PIECES)),
            pltpu.SemaphoreType.DMA(shape),
            pltpu.SemaphoreType.DMA(shape),
        ] + extra,
        compiler_params=pltpu.CompilerParams(
            collective_id=0, has_side_effects=True, vmem_limit_bytes=LIMIT
        ),
    )(density)
    return panels.reshape((-1,) + turned[1:]), shared


def live_list(columns, rows, width, group_size, span):
    total, stored = columns.shape
    base = lax.axis_index("row") * rows
    first = lax.axis_index("col") * group_size
    own = lax.dynamic_slice_in_dim(columns, base, rows, 0)
    wanted = lax.dynamic_slice_in_dim(own, first, group_size, 1)
    group = lax.dynamic_slice_in_dim(columns, first, group_size, 1)
    candidates = jnp.take(group, own, axis=0)
    distance = jnp.mod(own - base + span * rows, total)
    equal = candidates[:, :, :, None] == wanted[:, None, None, :]
    slots = jnp.arange(group_size, dtype=jnp.int32)
    live = jnp.any(equal, axis=-1)
    place = jnp.sum(jnp.where(equal, slots, 0), axis=-1)
    inner = jnp.mod(jnp.arange(stored, dtype=jnp.int32) - first, stored)[None, :, None]
    odd = jnp.mod(inner, 2)
    flip = (jnp.mod(distance[:, :, None], 2) != odd).astype(jnp.int32)
    code = (distance[:, :, None] // 2) * 256 + slots
    code = (code * 256 + inner // 2) * 16 + place
    code = code * 4 + flip * 2 + odd
    flat = live.reshape(rows, stored * group_size)
    code = code.reshape(rows, stored * group_size)
    order = jnp.cumsum(flat.astype(jnp.int32), axis=1)
    ranks = jnp.arange(1, stored * group_size + 1, dtype=jnp.int32)
    chosen = flat[:, None, :] & (order[:, None, :] == ranks[None, :, None])
    packed = jnp.sum(jnp.where(chosen, code[:, None, :] + 1, 0), axis=-1)
    return order[:, -1], packed - 1


def fill_halves(halves_ref, width):
    lane = lax.broadcasted_iota(jnp.int32, (width, 2 * width), 1)
    high = jnp.where(lane >= width, 1.0, 0.0)
    halves_ref[...] = jnp.zeros(halves_ref.shape, halves_ref.dtype)
    for flip in range(2):
        for odd in range(2):
            halves_ref[2 * flip + odd, flip] = (high if odd else 1.0 - high).astype(halves_ref.dtype)


def multiply(right_ref, left_refs):
    depth = left_refs[0].shape[-1]
    total, start = None, 0
    for left_ref in left_refs:
        part = lax.dot_general(
            right_ref[:, start:start + depth], left_ref[...], (((1,), (1,)), ((), ())),
            preferred_element_type=jnp.float32,
        )
        total = part if total is None else total + part
        start += depth
    return total.T


def first_kernel(stored, group_size, width, count_ref, code_ref, panels_ref, left_ref, rights, square_ref, halves_ref):
    rows, depth, _ = rights.shape
    fill_halves(halves_ref, width)

    def one_row(row, carry):
        right_ref = rights.at[row]
        right_ref[...] = jnp.zeros(right_ref.shape, right_ref.dtype)
        assemble(count_ref, code_ref, panels_ref, halves_ref, row, right_ref, width)
        total = multiply(right_ref, [left_ref.at[group, row] for group in range(left_ref.shape[0])])
        square_ref[row] = total.astype(square_ref.dtype)
        return carry

    lax.fori_loop(0, rows, one_row, 0)


def second_kernel(own_ref, shared_ref, rights, out_hbm, out_ref, out_sem):
    rows = own_ref.shape[0]

    def leave(row):
        return pltpu.make_async_copy(out_ref.at[row], out_hbm.at[row], out_sem.at[row])

    def one_row(row, carry):
        left = [own_ref.at[row]] + [shared_ref.at[step, row] for step in range(shared_ref.shape[0])]
        out_ref[row] = 3.0 * own_ref[row].astype(jnp.float32) - 2.0 * multiply(rights.at[row], left)
        leave(row).start()
        return carry

    def done(row, carry):
        leave(row).wait()
        return carry

    lax.fori_loop(0, rows, one_row, 0)
    lax.fori_loop(0, rows, done, 0)


def assemble(count_ref, code_ref, panels_ref, halves_ref, row, right_ref, width):
    def one(entry, carry):
        pieces = []
        for part in range(UNROLL):
            raw = code_ref[row, entry * UNROLL + part]
            kind = jnp.where(raw >= 0, raw & 3, 4)
            code = jnp.maximum(raw, 0)
            place, inner = (code >> 2) & 15, (code >> 6) & 255
            slot, source = (code >> 14) & 255, code >> 22
            value = panels_ref[source, pl.ds(pl.multiple_of(slot * width, width), width), :]
            swapped = jnp.concatenate([value[:, width:], value[:, :width]], axis=1)
            keep, turn_over = halves_ref[kind, 0], halves_ref[kind, 1]
            pieces.append((inner, place, value * keep + swapped * turn_over))
        for inner, place, value in pieces:
            lanes = pl.ds(pl.multiple_of(inner * 2 * width, 2 * width), 2 * width)
            lines = pl.ds(pl.multiple_of(place * width, width), width)
            right_ref[lines, lanes] += value
        return carry

    lax.fori_loop(0, lax.div(count_ref[row] + UNROLL - 1, UNROLL), one, 0)


def shards(density, columns):
    rows, width, depth = density.shape
    total, stored = columns.shape
    group_size = depth // width
    groups = stored // group_size
    span = -(-REACH // rows)
    count, codes = live_list(columns, rows, width, group_size, span)
    size = lax.axis_size("row")
    planes = (size, groups, span) == (16, 2, 3)
    panels, left = fetch(density, groups, size, span, planes)
    inside = pl.BlockSpec(memory_space=pltpu.VMEM)
    scalars = pl.BlockSpec(memory_space=pltpu.SMEM)
    right, square = pl.pallas_call(
        functools.partial(first_kernel, stored, group_size, width),
        in_specs=[scalars, scalars, inside, inside],
        out_specs=[inside, inside],
        out_shape=[
            jax.ShapeDtypeStruct((rows, depth, stored * width), density.dtype),
            jax.ShapeDtypeStruct(density.shape, density.dtype),
        ],
        scratch_shapes=[pltpu.VMEM((5, 2, width, 2 * width), density.dtype)],
        compiler_params=pltpu.CompilerParams(vmem_limit_bytes=LIMIT),
    )(count, codes, panels, left)
    return pl.pallas_call(
        second_kernel,
        in_specs=[inside, inside, inside],
        out_specs=pl.BlockSpec(memory_space=pl.ANY),
        out_shape=jax.ShapeDtypeStruct(density.shape, jnp.float32),
        scratch_shapes=[
            pltpu.VMEM(density.shape, jnp.float32),
            pltpu.SemaphoreType.DMA((rows,)),
        ],
        compiler_params=pltpu.CompilerParams(vmem_limit_bytes=LIMIT),
    )(square, exchange(square, groups, 1), right)


def solution(mesh):
    placed = (P("row", None, "col"), P())
    return jax.shard_map(
        shards, mesh=mesh, in_specs=placed, out_specs=P("row", None, "col"), check_vma=False
    )
```

```python
import functools

import jax
import jax.numpy as jnp
from jax import lax
from jax.experimental import pallas as pl
from jax.experimental.pallas import tpu as pltpu
from jax.sharding import PartitionSpec as P

REACH = 48
UNROLL = 8
PIECES = 8
LIMIT = 8 * 1024 * 1024


def greet(devices):
    barrier = pltpu.get_barrier_semaphore()
    for device in devices:
        pl.semaphore_signal(barrier, inc=1, device_id=device, device_id_type=pl.DeviceIdType.MESH)
    pl.semaphore_wait(barrier, len(devices))


def col_peers(groups):
    return [{"col": lax.rem(lax.axis_index("col") + step, groups)} for step in range(1, groups)]


def share_with_peers(groups, block, shared, first, send_sem, recv_sem):
    copies = []
    chunks = send_sem.shape[1]
    depth = block.shape[0] // chunks
    for step, peer in enumerate(col_peers(groups)):
        for chunk in range(chunks):
            lines = pl.ds(chunk * depth, depth)
            copies.append(pltpu.make_async_remote_copy(
                src_ref=block.at[lines], dst_ref=shared.at[first + groups - 2 - step, lines],
                send_sem=send_sem.at[step, chunk], recv_sem=recv_sem.at[step, chunk],
                device_id=peer, device_id_type=pl.DeviceIdType.MESH,
            ))
            copies[-1].start()
    return copies


def exchange_kernel(groups, block, shared, send_sem, recv_sem):
    greet(col_peers(groups))
    for copy in share_with_peers(groups, block, shared, 0, send_sem, recv_sem):
        copy.wait()


def exchange(block, groups, collective_id):
    return pl.pallas_call(
        functools.partial(exchange_kernel, groups),
        in_specs=[pl.BlockSpec(memory_space=pltpu.VMEM)],
        out_specs=pl.BlockSpec(memory_space=pltpu.VMEM),
        out_shape=jax.ShapeDtypeStruct((groups - 1,) + block.shape, block.dtype),
        scratch_shapes=[pltpu.SemaphoreType.DMA((groups - 1, PIECES))] * 2,
        compiler_params=pltpu.CompilerParams(
            collective_id=collective_id, has_side_effects=True, vmem_limit_bytes=LIMIT
        ),
    )(block)


def turn(block, turned, pair):
    wide = jnp.concatenate([block[2 * pair], block[2 * pair + 1]], axis=0)
    turned[pair] = wide.T


def direct_kernel(groups, size, span, block, panels, shared, turned, own_sem, col_send, col_recv, send_sem, recv_sem):
    me = lax.axis_index("row")
    offsets = [d for d in range(-span, span + 1) if d != 0]
    greet([{"row": lax.rem(me + d + size, size)} for d in offsets] + col_peers(groups))
    copies = share_with_peers(groups, block, shared, 1, col_send, col_recv)
    shared[0] = block[...]
    for pair in range(turned.shape[0]):
        turn(block, turned, pair)
    own = pltpu.make_async_copy(turned, panels.at[span], own_sem)
    own.start()
    for step, d in enumerate(offsets):
        copies.append(pltpu.make_async_remote_copy(
            src_ref=turned, dst_ref=panels.at[span - d], send_sem=send_sem.at[step], recv_sem=recv_sem.at[step],
            device_id={"row": lax.rem(me + d + size, size)}, device_id_type=pl.DeviceIdType.MESH,
        ))
        copies[-1].start()
    for copy in copies:
        copy.wait()
    own.wait()


def relay_kernel(groups, size, chunks, block, panels, shared, turned, own_sem, col_send, col_recv, send_sem, recv_sem, held, up_send, up_recv):
    me = lax.axis_index("row")
    x_step = 1 - 2 * lax.rem(me, 2)
    y_step = 2 - 4 * lax.rem(lax.div(me, 2), 2)
    steps = [x_step, y_step, x_step + y_step]
    x_near, y_near = me + x_step, me + y_step
    above, below = lax.rem(me + 4, size), lax.rem(me + size - 4, size)
    greet([{"row": d} for d in (x_near, y_near, above, below)] + col_peers(groups))
    others = []
    depth = turned.shape[0] // chunks

    def send(kind, chunk, source, slot, device):
        lines = pl.ds(chunk * depth, depth)
        copy = pltpu.make_async_remote_copy(
            src_ref=source.at[lines], dst_ref=panels.at[slot, lines],
            send_sem=send_sem.at[kind, chunk], recv_sem=recv_sem.at[kind, chunk],
            device_id={"row": device}, device_id_type=pl.DeviceIdType.MESH,
        )
        copy.start()
        others.append(copy)
        return copy

    def from_held(kind, chunk, way, slot, device):
        lines = pl.ds(chunk * depth, depth)
        copy = pltpu.make_async_remote_copy(
            src_ref=held.at[way, chunk // 2], dst_ref=panels.at[slot, lines],
            send_sem=send_sem.at[kind, chunk], recv_sem=recv_sem.at[kind, chunk],
            device_id={"row": device}, device_id_type=pl.DeviceIdType.MESH,
        )
        copy.start()
        others.append(copy)
        return copy

    def pass_on(kind, chunk):
        step = steps[kind]
        sign = jnp.where(step > 0, 1, -1)
        target = lax.rem(me + 4 * sign + size, size)
        late.append(send(3 + kind, chunk, panels.at[3 + step], 3 + step - 4 * sign, target))

    place = lax.rem(me, 4)
    x_sign, y_sign = x_step, lax.div(y_step, 2)
    x_held = lax.div(1 + x_sign, 2)
    y_held = lax.div(1 + y_sign, 2)

    def level(way, chunk):
        lines = pl.ds(chunk * depth, depth)
        return pltpu.make_async_remote_copy(
            src_ref=turned.at[lines], dst_ref=held.at[way, chunk // 2],
            send_sem=up_send.at[way, chunk // 2], recv_sem=up_recv.at[way, chunk // 2],
            device_id={"row": above if way == 0 else below}, device_id_type=pl.DeviceIdType.MESH,
        )

    def on_level(chunk, act):
        @pl.when(place > 0)
        def _():
            act(level(0, chunk))

        @pl.when(place < 3)
        def _():
            act(level(1, chunk))

    late, arriving = [], []
    for chunk in range(chunks):
        for pair in range(chunk * depth, (chunk + 1) * depth):
            turn(block, turned, pair)
        if chunk % 2 == 0:
            on_level(chunk, lambda copy: copy.start())
        arriving.append((
            send(0, chunk, turned, 3 - x_step, x_near),
            send(1, chunk, turned, 3 - y_step, y_near),
        ))
    own = pltpu.make_async_copy(turned, panels.at[3], own_sem)
    own.start()
    col_copies = share_with_peers(groups, block, shared, 1, col_send, col_recv)
    shared[0] = block[...]
    corner, spread = {}, {}
    lag = 2
    for chunk in range(chunks + lag):
        if chunk < chunks:
            by_y = chunk % 4 != 1
            arriving[chunk][0].wait_recv()
            if by_y:
                corner[chunk] = send(2, chunk, panels.at[3 + x_step], 3 + x_step - y_step, y_near)
            if chunk % 2 == 1:
                pass_on(0, chunk)
            arriving[chunk][1].wait_recv()
            if not by_y:
                corner[chunk] = send(2, chunk, panels.at[3 + y_step], 3 + y_step - x_step, x_near)
            if chunk % 2 == 1:
                pass_on(1, chunk)
            else:
                on_level(chunk, lambda copy: copy.wait_recv())
                late.append(from_held(3, chunk, x_held, 3 - x_step + 4 * x_sign, x_near))
                spread[chunk] = from_held(4, chunk, y_held, 3 - y_step + 4 * y_sign, y_near)
        done = chunk - lag
        if done >= 0:
            corner[done].wait_recv()
            if done % 2 == 1:
                pass_on(2, done)
            else:
                spread[done].wait_recv()
                slot = 3 + y_step - 4 * y_sign
                late.append(send(5, done, panels.at[slot], slot - x_step, x_near))
    for copy in late:
        copy.wait_recv()
    for chunk in range(0, chunks, 2):
        on_level(chunk, lambda copy: copy.wait_send())
    for copy in others:
        copy.wait_send()
    for copy in col_copies:
        copy.wait()
    own.wait()


def fetch(density, groups, size, span, planes):
    chunks = 8
    if planes:
        body, shape = functools.partial(relay_kernel, groups, size, chunks), (6, chunks)
    else:
        body, shape = functools.partial(direct_kernel, groups, size, span), (2 * span,)
    inside = pl.BlockSpec(memory_space=pltpu.VMEM)
    rows, width, depth = density.shape
    turned = (rows // 2, depth, 2 * width)
    extra = []
    if planes:
        extra = [
            pltpu.VMEM((2, chunks // 2, rows // 2 // chunks, depth, 2 * width), density.dtype),
            pltpu.SemaphoreType.DMA((2, chunks // 2)),
            pltpu.SemaphoreType.DMA((2, chunks // 2)),
        ]
    panels, shared = pl.pallas_call(
        body,
        in_specs=[inside],
        out_specs=[inside, inside],
        out_shape=[
            jax.ShapeDtypeStruct((2 * span + 1,) + turned, density.dtype),
            jax.ShapeDtypeStruct((groups,) + density.shape, density.dtype),
        ],
        scratch_shapes=[
            pltpu.VMEM(turned, density.dtype),
            pltpu.SemaphoreType.DMA,
            pltpu.SemaphoreType.DMA((groups - 1, PIECES)),
            pltpu.SemaphoreType.DMA((groups - 1, PIECES)),
            pltpu.SemaphoreType.DMA(shape),
            pltpu.SemaphoreType.DMA(shape),
        ] + extra,
        compiler_params=pltpu.CompilerParams(
            collective_id=0, has_side_effects=True, vmem_limit_bytes=LIMIT
        ),
    )(density)
    return panels.reshape((-1,) + turned[1:]), shared


def live_list(columns, rows, width, group_size, span):
    total, stored = columns.shape
    base = lax.axis_index("row") * rows
    first = lax.axis_index("col") * group_size
    own = lax.dynamic_slice_in_dim(columns, base, rows, 0)
    wanted = lax.dynamic_slice_in_dim(own, first, group_size, 1)
    group = lax.dynamic_slice_in_dim(columns, first, group_size, 1)
    candidates = jnp.take(group, own, axis=0)
    distance = jnp.mod(own - base + span * rows, total)
    equal = candidates[:, :, :, None] == wanted[:, None, None, :]
    slots = jnp.arange(group_size, dtype=jnp.int32)
    live = jnp.any(equal, axis=-1)
    place = jnp.sum(jnp.where(equal, slots, 0), axis=-1)
    inner = jnp.mod(jnp.arange(stored, dtype=jnp.int32) - first, stored)[None, :, None]
    odd = jnp.mod(inner, 2)
    flip = (jnp.mod(distance[:, :, None], 2) != odd).astype(jnp.int32)
    code = (distance[:, :, None] // 2) * 256 + slots
    code = (code * 256 + inner // 2) * 16 + place
    code = code * 4 + flip * 2 + odd
    length = stored * group_size // 2

    def by_parity(values):
        return values.reshape(rows, stored // 2, 2, group_size).transpose(0, 2, 1, 3).reshape(rows, 2, length)

    flat, code = by_parity(live), by_parity(code)
    order = jnp.cumsum(flat.astype(jnp.int32), axis=2)
    ranks = jnp.arange(1, length + 1, dtype=jnp.int32)
    wanted_rank = jnp.minimum(ranks, order[:, :, -1:])
    chosen = flat[:, :, None, :] & (order[:, :, None, :] == wanted_rank[:, :, :, None])
    packed = jnp.sum(jnp.where(chosen, code[:, :, None, :], 0), axis=-1)
    return order[:, :, -1].reshape(-1), packed.reshape(2 * rows, length)


def fill_halves(halves_ref, width):
    lane = lax.broadcasted_iota(jnp.int32, (width, 2 * width), 1)
    high = jnp.where(lane >= width, 1.0, 0.0)
    halves_ref[...] = jnp.zeros(halves_ref.shape, halves_ref.dtype)
    for flip in range(2):
        for odd in range(2):
            halves_ref[2 * flip + odd, flip] = (high if odd else 1.0 - high).astype(halves_ref.dtype)


def multiply(right_ref, left_refs):
    depth = left_refs[0].shape[-1]
    total, start = None, 0
    for left_ref in left_refs:
        part = lax.dot_general(
            right_ref[:, start:start + depth], left_ref[...], (((1,), (1,)), ((), ())),
            preferred_element_type=jnp.float32,
        )
        total = part if total is None else total + part
        start += depth
    return total.T


def first_kernel(stored, group_size, width, count_ref, code_ref, panels_ref, left_ref, rights, square_ref, halves_ref):
    rows, depth, _ = rights.shape
    fill_halves(halves_ref, width)

    def one_row(row, carry):
        right_ref = rights.at[row]
        right_ref[...] = jnp.zeros(right_ref.shape, right_ref.dtype)
        assemble(count_ref, code_ref, panels_ref, halves_ref, row, right_ref, width)
        total = multiply(right_ref, [left_ref.at[group, row] for group in range(left_ref.shape[0])])
        square_ref[row] = total.astype(square_ref.dtype)
        return carry

    lax.fori_loop(0, rows, one_row, 0)


def second_kernel(own_ref, shared_ref, rights, out_hbm, out_ref, out_sem):
    rows = own_ref.shape[0]

    def leave(row):
        return pltpu.make_async_copy(out_ref.at[row], out_hbm.at[row], out_sem.at[row])

    def one_row(row, carry):
        left = [own_ref.at[row]] + [shared_ref.at[step, row] for step in range(shared_ref.shape[0])]
        out_ref[row] = 3.0 * own_ref[row].astype(jnp.float32) - 2.0 * multiply(rights.at[row], left)
        leave(row).start()
        return carry

    def done(row, carry):
        leave(row).wait()
        return carry

    lax.fori_loop(0, rows, one_row, 0)
    lax.fori_loop(0, rows, done, 0)


def assemble(count_ref, code_ref, panels_ref, halves_ref, row, right_ref, width):
    for parity in range(2):
        line = 2 * row + parity

        def one(entry, carry):
            pieces = []
            for part in range(UNROLL):
                code = code_ref[line, entry * UNROLL + part]
                kind = code & 3
                place, inner = (code >> 2) & 15, (code >> 6) & 255
                slot, source = (code >> 14) & 255, code >> 22
                value = panels_ref[source, pl.ds(pl.multiple_of(slot * width, width), width), :]
                swapped = jnp.concatenate([value[:, width:], value[:, :width]], axis=1)
                value = value * halves_ref[kind, 0] + swapped * halves_ref[kind, 1]
                lanes = pl.ds(pl.multiple_of(inner * 2 * width, 2 * width), 2 * width)
                lines = pl.ds(pl.multiple_of(place * width, width), width)
                if parity == 1:
                    value = value + right_ref[lines, lanes]
                pieces.append((lines, lanes, value))
            for lines, lanes, value in pieces:
                right_ref[lines, lanes] = value
            return carry

        lax.fori_loop(0, lax.div(count_ref[line] + UNROLL - 1, UNROLL), one, 0)


def shards(density, columns):
    rows, width, depth = density.shape
    total, stored = columns.shape
    group_size = depth // width
    groups = stored // group_size
    span = -(-REACH // rows)
    count, codes = live_list(columns, rows, width, group_size, span)
    size = lax.axis_size("row")
    planes = (size, groups, span) == (16, 2, 3)
    panels, left = fetch(density, groups, size, span, planes)
    inside = pl.BlockSpec(memory_space=pltpu.VMEM)
    scalars = pl.BlockSpec(memory_space=pltpu.SMEM)
    right, square = pl.pallas_call(
        functools.partial(first_kernel, stored, group_size, width),
        in_specs=[scalars, scalars, inside, inside],
        out_specs=[inside, inside],
        out_shape=[
            jax.ShapeDtypeStruct((rows, depth, stored * width), density.dtype),
            jax.ShapeDtypeStruct(density.shape, density.dtype),
        ],
        scratch_shapes=[pltpu.VMEM((4, 2, width, 2 * width), density.dtype)],
        compiler_params=pltpu.CompilerParams(vmem_limit_bytes=LIMIT),
    )(count, codes, panels, left)
    return pl.pallas_call(
        second_kernel,
        in_specs=[inside, inside, inside],
        out_specs=pl.BlockSpec(memory_space=pl.ANY),
        out_shape=jax.ShapeDtypeStruct(density.shape, jnp.float32),
        scratch_shapes=[
            pltpu.VMEM(density.shape, jnp.float32),
            pltpu.SemaphoreType.DMA((rows,)),
        ],
        compiler_params=pltpu.CompilerParams(vmem_limit_bytes=LIMIT),
    )(square, exchange(square, groups, 1), right)


def solution(mesh):
    placed = (P("row", None, "col"), P())
    return jax.shard_map(
        shards, mesh=mesh, in_specs=placed, out_specs=P("row", None, "col"), check_vma=False
    )
```

```python
import functools

import jax
import jax.numpy as jnp
from jax import lax
from jax.experimental import pallas as pl
from jax.experimental.pallas import tpu as pltpu
from jax.sharding import PartitionSpec as P

REACH = 48
UNROLL = 8
PIECES = 8
CHUNKS = 8
Z_FIRST = (0, 1, 3, 5, 7)
LIMIT = 8 * 1024 * 1024


def greet(devices):
    barrier = pltpu.get_barrier_semaphore()
    for device in devices:
        pl.semaphore_signal(barrier, inc=1, device_id=device, device_id_type=pl.DeviceIdType.MESH)
    pl.semaphore_wait(barrier, len(devices))


def col_peers(groups):
    return [{"col": lax.rem(lax.axis_index("col") + step, groups)} for step in range(1, groups)]


def share_with_peers(groups, block, shared, first, send_sem, recv_sem):
    copies = []
    chunks = send_sem.shape[1]
    depth = block.shape[0] // chunks
    for step, peer in enumerate(col_peers(groups)):
        for chunk in range(chunks):
            lines = pl.ds(chunk * depth, depth)
            copies.append(pltpu.make_async_remote_copy(
                src_ref=block.at[lines], dst_ref=shared.at[first + groups - 2 - step, lines],
                send_sem=send_sem.at[step, chunk], recv_sem=recv_sem.at[step, chunk],
                device_id=peer, device_id_type=pl.DeviceIdType.MESH,
            ))
            copies[-1].start()
    return copies


def exchange_kernel(groups, block, shared, send_sem, recv_sem):
    greet(col_peers(groups))
    for copy in share_with_peers(groups, block, shared, 0, send_sem, recv_sem):
        copy.wait()


def exchange(block, groups, collective_id):
    return pl.pallas_call(
        functools.partial(exchange_kernel, groups),
        in_specs=[pl.BlockSpec(memory_space=pltpu.VMEM)],
        out_specs=pl.BlockSpec(memory_space=pltpu.VMEM),
        out_shape=jax.ShapeDtypeStruct((groups - 1,) + block.shape, block.dtype),
        scratch_shapes=[pltpu.SemaphoreType.DMA((groups - 1, PIECES))] * 2,
        compiler_params=pltpu.CompilerParams(
            collective_id=collective_id, has_side_effects=True, vmem_limit_bytes=LIMIT
        ),
    )(block)


def turn(block, turned, pair):
    wide = jnp.concatenate([block[2 * pair], block[2 * pair + 1]], axis=0)
    turned[pair] = wide.T


def direct_kernel(groups, size, span, block, panels, shared, blank, turned, own_sem, col_send, col_recv, send_sem, recv_sem):
    me = lax.axis_index("row")
    offsets = [d for d in range(-span, span + 1) if d != 0]
    greet([{"row": lax.rem(me + d + size, size)} for d in offsets] + col_peers(groups))
    copies = share_with_peers(groups, block, shared, 1, col_send, col_recv)
    shared[0] = block[...]
    for pair in range(turned.shape[0]):
        turn(block, turned, pair)
    own = pltpu.make_async_copy(turned, panels.at[span], own_sem)
    own.start()
    for step, d in enumerate(offsets):
        copies.append(pltpu.make_async_remote_copy(
            src_ref=turned, dst_ref=panels.at[span - d], send_sem=send_sem.at[step], recv_sem=recv_sem.at[step],
            device_id={"row": lax.rem(me + d + size, size)}, device_id_type=pl.DeviceIdType.MESH,
        ))
        copies[-1].start()
    blank[...] = jnp.zeros(blank.shape, blank.dtype)
    for copy in copies:
        copy.wait()
    own.wait()


def relay_kernel(groups, size, chunks, block, panels, shared, blank, turned, own_sem, col_send, col_recv, send_sem, recv_sem, held, up_send, up_recv):
    me = lax.axis_index("row")
    x_step = 1 - 2 * lax.rem(me, 2)
    y_step = 2 - 4 * lax.rem(lax.div(me, 2), 2)
    steps = [x_step, y_step, x_step + y_step]
    x_near, y_near = me + x_step, me + y_step
    above, below = lax.rem(me + 4, size), lax.rem(me + size - 4, size)
    greet([{"row": d} for d in (x_near, y_near, above, below)] + col_peers(groups))
    others = []
    depth = turned.shape[0] // chunks

    def send(kind, chunk, source, slot, device):
        lines = pl.ds(chunk * depth, depth)
        copy = pltpu.make_async_remote_copy(
            src_ref=source.at[lines], dst_ref=panels.at[slot, lines],
            send_sem=send_sem.at[kind, chunk], recv_sem=recv_sem.at[kind, chunk],
            device_id={"row": device}, device_id_type=pl.DeviceIdType.MESH,
        )
        copy.start()
        others.append(copy)
        return copy

    def from_held(kind, chunk, way, slot, device):
        lines = pl.ds(chunk * depth, depth)
        copy = pltpu.make_async_remote_copy(
            src_ref=held.at[way, Z_FIRST.index(chunk)], dst_ref=panels.at[slot, lines],
            send_sem=send_sem.at[kind, chunk], recv_sem=recv_sem.at[kind, chunk],
            device_id={"row": device}, device_id_type=pl.DeviceIdType.MESH,
        )
        copy.start()
        others.append(copy)
        return copy

    def pass_on(kind, chunk):
        step = steps[kind]
        sign = jnp.where(step > 0, 1, -1)
        target = lax.rem(me + 4 * sign + size, size)
        late.append(send(3 + kind, chunk, panels.at[3 + step], 3 + step - 4 * sign, target))

    place = lax.rem(me, 4)
    x_sign, y_sign = x_step, lax.div(y_step, 2)
    x_held = lax.div(1 + x_sign, 2)
    y_held = lax.div(1 + y_sign, 2)

    def level(way, chunk):
        lines = pl.ds(chunk * depth, depth)
        return pltpu.make_async_remote_copy(
            src_ref=turned.at[lines], dst_ref=held.at[way, Z_FIRST.index(chunk)],
            send_sem=up_send.at[way, Z_FIRST.index(chunk)], recv_sem=up_recv.at[way, Z_FIRST.index(chunk)],
            device_id={"row": above if way == 0 else below}, device_id_type=pl.DeviceIdType.MESH,
        )

    def on_level(chunk, act):
        @pl.when(place > 0)
        def _():
            act(level(0, chunk))

        @pl.when(place < 3)
        def _():
            act(level(1, chunk))

    late, arriving = [], []
    for chunk in range(chunks):
        for pair in range(chunk * depth, (chunk + 1) * depth):
            turn(block, turned, pair)
        if chunk in Z_FIRST:
            on_level(chunk, lambda copy: copy.start())
        arriving.append((
            send(0, chunk, turned, 3 - x_step, x_near),
            send(1, chunk, turned, 3 - y_step, y_near),
        ))
    own = pltpu.make_async_copy(turned, panels.at[3], own_sem)
    own.start()
    col_copies = share_with_peers(groups, block, shared, 1, col_send, col_recv)
    shared[0] = block[...]
    corner, spread = {}, {}
    lag = 2
    for chunk in range(chunks + lag):
        if chunk < chunks:
            by_y = chunk != 4
            arriving[chunk][0].wait_recv()
            if by_y:
                corner[chunk] = send(2, chunk, panels.at[3 + x_step], 3 + x_step - y_step, y_near)
            if chunk not in Z_FIRST:
                pass_on(0, chunk)
            arriving[chunk][1].wait_recv()
            if not by_y:
                corner[chunk] = send(2, chunk, panels.at[3 + y_step], 3 + y_step - x_step, x_near)
            if chunk not in Z_FIRST:
                pass_on(1, chunk)
            else:
                on_level(chunk, lambda copy: copy.wait_recv())
                late.append(from_held(3, chunk, x_held, 3 - x_step + 4 * x_sign, x_near))
                spread[chunk] = from_held(4, chunk, y_held, 3 - y_step + 4 * y_sign, y_near)
            lines = blank.shape[0] // chunks
            for row in range(chunk * lines, (chunk + 1) * lines):
                blank[row] = jnp.zeros(blank.shape[1:], blank.dtype)
        done = chunk - lag
        if done >= 0:
            corner[done].wait_recv()
            if done not in Z_FIRST:
                pass_on(2, done)
            else:
                spread[done].wait_recv()
                slot = 3 + y_step - 4 * y_sign
                late.append(send(5, done, panels.at[slot], slot - x_step, x_near))
    for copy in late:
        copy.wait_recv()
    for chunk in Z_FIRST:
        on_level(chunk, lambda copy: copy.wait_send())
    for copy in others:
        copy.wait_send()
    for copy in col_copies:
        copy.wait()
    own.wait()


def fetch(density, groups, size, span, planes):
    chunks = CHUNKS
    if planes:
        body, shape = functools.partial(relay_kernel, groups, size, chunks), (6, chunks)
    else:
        body, shape = functools.partial(direct_kernel, groups, size, span), (2 * span,)
    inside = pl.BlockSpec(memory_space=pltpu.VMEM)
    rows, width, depth = density.shape
    turned = (rows // 2, depth, 2 * width)
    extra = []
    if planes:
        extra = [
            pltpu.VMEM((2, len(Z_FIRST), rows // 2 // chunks, depth, 2 * width), density.dtype),
            pltpu.SemaphoreType.DMA((2, len(Z_FIRST))),
            pltpu.SemaphoreType.DMA((2, len(Z_FIRST))),
        ]
    panels, shared, blank = pl.pallas_call(
        body,
        in_specs=[inside],
        out_specs=[inside, inside, inside],
        out_shape=[
            jax.ShapeDtypeStruct((2 * span + 1,) + turned, density.dtype),
            jax.ShapeDtypeStruct((groups,) + density.shape, density.dtype),
            jax.ShapeDtypeStruct((rows, depth, groups * depth), density.dtype),
        ],
        scratch_shapes=[
            pltpu.VMEM(turned, density.dtype),
            pltpu.SemaphoreType.DMA,
            pltpu.SemaphoreType.DMA((groups - 1, PIECES)),
            pltpu.SemaphoreType.DMA((groups - 1, PIECES)),
            pltpu.SemaphoreType.DMA(shape),
            pltpu.SemaphoreType.DMA(shape),
        ] + extra,
        compiler_params=pltpu.CompilerParams(
            collective_id=0, has_side_effects=True, vmem_limit_bytes=LIMIT
        ),
    )(density)
    return panels.reshape((-1,) + turned[1:]), shared, blank


def live_list(columns, rows, width, group_size, span):
    total, stored = columns.shape
    base = lax.axis_index("row") * rows
    first = lax.axis_index("col") * group_size
    own = lax.dynamic_slice_in_dim(columns, base, rows, 0)
    wanted = lax.dynamic_slice_in_dim(own, first, group_size, 1)
    group = lax.dynamic_slice_in_dim(columns, first, group_size, 1)
    candidates = jnp.take(group, own, axis=0)
    distance = jnp.mod(own - base + span * rows, total)
    equal = candidates[:, :, :, None] == wanted[:, None, None, :]
    slots = jnp.arange(group_size, dtype=jnp.int32)
    live = jnp.any(equal, axis=-1)
    place = jnp.sum(jnp.where(equal, slots, 0), axis=-1)
    inner = jnp.mod(jnp.arange(stored, dtype=jnp.int32) - first, stored)[None, :, None]
    odd = jnp.mod(inner, 2)
    flip = (jnp.mod(distance[:, :, None], 2) != odd).astype(jnp.int32)
    code = (distance[:, :, None] // 2) * 256 + slots
    code = (code * 256 + inner // 2) * 16 + place
    code = code * 4 + flip * 2 + odd
    length = stored * group_size // 2

    def by_parity(values):
        return values.reshape(rows, stored // 2, 2, group_size).transpose(0, 2, 1, 3).reshape(rows, 2, length)

    flat, code = by_parity(live), by_parity(code)
    order = jnp.cumsum(flat.astype(jnp.int32), axis=2)
    ranks = jnp.arange(1, length + 1, dtype=jnp.int32)
    wanted_rank = jnp.minimum(ranks, order[:, :, -1:])
    chosen = flat[:, :, None, :] & (order[:, :, None, :] == wanted_rank[:, :, :, None])
    packed = jnp.sum(jnp.where(chosen, code[:, :, None, :], 0), axis=-1)
    return order[:, :, -1].reshape(-1), packed.reshape(2 * rows, length)


def fill_halves(halves_ref, width):
    lane = lax.broadcasted_iota(jnp.int32, (width, 2 * width), 1)
    high = jnp.where(lane >= width, 1.0, 0.0)
    halves_ref[...] = jnp.zeros(halves_ref.shape, halves_ref.dtype)
    for flip in range(2):
        for odd in range(2):
            halves_ref[2 * flip + odd, flip] = (high if odd else 1.0 - high).astype(halves_ref.dtype)


def multiply(right_ref, left_refs):
    depth = left_refs[0].shape[-1]
    total, start = None, 0
    for left_ref in left_refs:
        part = lax.dot_general(
            right_ref[:, start:start + depth], left_ref[...], (((1,), (1,)), ((), ())),
            preferred_element_type=jnp.float32,
        )
        total = part if total is None else total + part
        start += depth
    return total.T


def first_kernel(stored, group_size, width, count_ref, code_ref, panels_ref, left_ref, blank_ref, rights, square_ref, halves_ref):
    del blank_ref
    rows = rights.shape[0]
    fill_halves(halves_ref, width)

    def one_row(row, carry):
        right_ref = rights.at[row]
        assemble(count_ref, code_ref, panels_ref, halves_ref, row, right_ref, width)
        total = multiply(right_ref, [left_ref.at[group, row] for group in range(left_ref.shape[0])])
        square_ref[row] = total.astype(square_ref.dtype)
        return carry

    lax.fori_loop(0, rows, one_row, 0)


def second_kernel(own_ref, shared_ref, rights, out_hbm, out_ref, out_sem):
    rows = own_ref.shape[0]

    def leave(row):
        return pltpu.make_async_copy(out_ref.at[row], out_hbm.at[row], out_sem.at[row])

    def one_row(row, carry):
        left = [own_ref.at[row]] + [shared_ref.at[step, row] for step in range(shared_ref.shape[0])]
        out_ref[row] = 3.0 * own_ref[row].astype(jnp.float32) - 2.0 * multiply(rights.at[row], left)
        leave(row).start()
        return carry

    def done(row, carry):
        leave(row).wait()
        return carry

    lax.fori_loop(0, rows, one_row, 0)
    lax.fori_loop(0, rows, done, 0)


def assemble(count_ref, code_ref, panels_ref, halves_ref, row, right_ref, width):
    for parity in range(2):
        line = 2 * row + parity

        def one(entry, carry):
            pieces = []
            for part in range(UNROLL):
                code = code_ref[line, entry * UNROLL + part]
                kind = code & 3
                place, inner = (code >> 2) & 15, (code >> 6) & 255
                slot, source = (code >> 14) & 255, code >> 22
                value = panels_ref[source, pl.ds(pl.multiple_of(slot * width, width), width), :]
                swapped = jnp.concatenate([value[:, width:], value[:, :width]], axis=1)
                value = value * halves_ref[kind, 0] + swapped * halves_ref[kind, 1]
                lanes = pl.ds(pl.multiple_of(inner * 2 * width, 2 * width), 2 * width)
                lines = pl.ds(pl.multiple_of(place * width, width), width)
                if parity == 1:
                    value = value + right_ref[lines, lanes]
                pieces.append((lines, lanes, value))
            for lines, lanes, value in pieces:
                right_ref[lines, lanes] = value
            return carry

        lax.fori_loop(0, lax.div(count_ref[line] + UNROLL - 1, UNROLL), one, 0)


def shards(density, columns):
    rows, width, depth = density.shape
    total, stored = columns.shape
    group_size = depth // width
    groups = stored // group_size
    span = -(-REACH // rows)
    count, codes = live_list(columns, rows, width, group_size, span)
    size = lax.axis_size("row")
    planes = (size, groups, span) == (16, 2, 3)
    panels, left, blank = fetch(density, groups, size, span, planes)
    inside = pl.BlockSpec(memory_space=pltpu.VMEM)
    scalars = pl.BlockSpec(memory_space=pltpu.SMEM)
    right, square = pl.pallas_call(
        functools.partial(first_kernel, stored, group_size, width),
        in_specs=[scalars, scalars, inside, inside, inside],
        input_output_aliases={4: 0},
        out_specs=[inside, inside],
        out_shape=[
            jax.ShapeDtypeStruct((rows, depth, stored * width), density.dtype),
            jax.ShapeDtypeStruct(density.shape, density.dtype),
        ],
        scratch_shapes=[pltpu.VMEM((4, 2, width, 2 * width), density.dtype)],
        compiler_params=pltpu.CompilerParams(vmem_limit_bytes=LIMIT),
    )(count, codes, panels, left, blank)
    return pl.pallas_call(
        second_kernel,
        in_specs=[inside, inside, inside],
        out_specs=pl.BlockSpec(memory_space=pl.ANY),
        out_shape=jax.ShapeDtypeStruct(density.shape, jnp.float32),
        scratch_shapes=[
            pltpu.VMEM(density.shape, jnp.float32),
            pltpu.SemaphoreType.DMA((rows,)),
        ],
        compiler_params=pltpu.CompilerParams(vmem_limit_bytes=LIMIT),
    )(square, exchange(square, groups, 1), right)


def solution(mesh):
    placed = (P("row", None, "col"), P())
    return jax.shard_map(
        shards, mesh=mesh, in_specs=placed, out_specs=P("row", None, "col"), check_vma=False
    )
```

```python
import functools

import jax
import jax.numpy as jnp
from jax import lax
from jax.experimental import pallas as pl
from jax.experimental.pallas import tpu as pltpu
from jax.sharding import PartitionSpec as P

REACH = 48
UNROLL = 8
PIECES = 8
LIMIT = 8 * 1024 * 1024


def greet(devices):
    barrier = pltpu.get_barrier_semaphore()
    for device in devices:
        pl.semaphore_signal(barrier, inc=1, device_id=device, device_id_type=pl.DeviceIdType.MESH)
    pl.semaphore_wait(barrier, len(devices))


def col_peers(groups):
    return [{"col": lax.rem(lax.axis_index("col") + step, groups)} for step in range(1, groups)]


def share_with_peers(groups, block, shared, first, send_sem, recv_sem):
    copies = []
    chunks = send_sem.shape[1]
    depth = block.shape[0] // chunks
    for step, peer in enumerate(col_peers(groups)):
        for chunk in range(chunks):
            lines = pl.ds(chunk * depth, depth)
            copies.append(pltpu.make_async_remote_copy(
                src_ref=block.at[lines], dst_ref=shared.at[first + groups - 2 - step, lines],
                send_sem=send_sem.at[step, chunk], recv_sem=recv_sem.at[step, chunk],
                device_id=peer, device_id_type=pl.DeviceIdType.MESH,
            ))
            copies[-1].start()
    return copies


def exchange_kernel(groups, block, shared, send_sem, recv_sem):
    greet(col_peers(groups))
    for copy in share_with_peers(groups, block, shared, 0, send_sem, recv_sem):
        copy.wait()


def exchange(block, groups, collective_id):
    return pl.pallas_call(
        functools.partial(exchange_kernel, groups),
        in_specs=[pl.BlockSpec(memory_space=pltpu.VMEM)],
        out_specs=pl.BlockSpec(memory_space=pltpu.VMEM),
        out_shape=jax.ShapeDtypeStruct((groups - 1,) + block.shape, block.dtype),
        scratch_shapes=[pltpu.SemaphoreType.DMA((groups - 1, PIECES))] * 2,
        compiler_params=pltpu.CompilerParams(
            collective_id=collective_id, has_side_effects=True, vmem_limit_bytes=LIMIT
        ),
    )(block)


def turn(block, turned, pair):
    wide = jnp.concatenate([block[2 * pair], block[2 * pair + 1]], axis=0)
    turned[pair] = wide.T


def direct_kernel(groups, size, span, block, panels, shared, turned, own_sem, col_send, col_recv, send_sem, recv_sem):
    me = lax.axis_index("row")
    offsets = [d for d in range(-span, span + 1) if d != 0]
    greet([{"row": lax.rem(me + d + size, size)} for d in offsets] + col_peers(groups))
    copies = share_with_peers(groups, block, shared, 1, col_send, col_recv)
    shared[0] = block[...]
    for pair in range(turned.shape[0]):
        turn(block, turned, pair)
    own = pltpu.make_async_copy(turned, panels.at[span], own_sem)
    own.start()
    for step, d in enumerate(offsets):
        copies.append(pltpu.make_async_remote_copy(
            src_ref=turned, dst_ref=panels.at[span - d], send_sem=send_sem.at[step], recv_sem=recv_sem.at[step],
            device_id={"row": lax.rem(me + d + size, size)}, device_id_type=pl.DeviceIdType.MESH,
        ))
        copies[-1].start()
    for copy in copies:
        copy.wait()
    own.wait()


def relay_kernel(groups, size, chunks, block, panels, shared, turned, own_sem, col_send, col_recv, send_sem, recv_sem, held, up_send, up_recv):
    me = lax.axis_index("row")
    x_step = 1 - 2 * lax.rem(me, 2)
    y_step = 2 - 4 * lax.rem(lax.div(me, 2), 2)
    steps = [x_step, y_step, x_step + y_step]
    x_near, y_near = me + x_step, me + y_step
    above, below = lax.rem(me + 4, size), lax.rem(me + size - 4, size)
    greet([{"row": d} for d in (x_near, y_near, above, below)] + col_peers(groups))
    others = []
    depth = turned.shape[0] // chunks

    def send(kind, chunk, source, slot, device):
        lines = pl.ds(chunk * depth, depth)
        copy = pltpu.make_async_remote_copy(
            src_ref=source.at[lines], dst_ref=panels.at[slot, lines],
            send_sem=send_sem.at[kind, chunk], recv_sem=recv_sem.at[kind, chunk],
            device_id={"row": device}, device_id_type=pl.DeviceIdType.MESH,
        )
        copy.start()
        others.append(copy)
        return copy

    def from_held(kind, chunk, way, slot, device):
        lines = pl.ds(chunk * depth, depth)
        copy = pltpu.make_async_remote_copy(
            src_ref=held.at[way, chunk // 2], dst_ref=panels.at[slot, lines],
            send_sem=send_sem.at[kind, chunk], recv_sem=recv_sem.at[kind, chunk],
            device_id={"row": device}, device_id_type=pl.DeviceIdType.MESH,
        )
        copy.start()
        others.append(copy)
        return copy

    def pass_on(kind, chunk):
        step = steps[kind]
        sign = jnp.where(step > 0, 1, -1)
        target = lax.rem(me + 4 * sign + size, size)
        late.append(send(3 + kind, chunk, panels.at[3 + step], 3 + step - 4 * sign, target))

    place = lax.rem(me, 4)
    x_sign, y_sign = x_step, lax.div(y_step, 2)
    x_held = lax.div(1 + x_sign, 2)
    y_held = lax.div(1 + y_sign, 2)

    def level(way, chunk):
        lines = pl.ds(chunk * depth, depth)
        return pltpu.make_async_remote_copy(
            src_ref=turned.at[lines], dst_ref=held.at[way, chunk // 2],
            send_sem=up_send.at[way, chunk // 2], recv_sem=up_recv.at[way, chunk // 2],
            device_id={"row": above if way == 0 else below}, device_id_type=pl.DeviceIdType.MESH,
        )

    def on_level(chunk, act):
        @pl.when(place > 0)
        def _():
            act(level(0, chunk))

        @pl.when(place < 3)
        def _():
            act(level(1, chunk))

    late, arriving = [], []
    for chunk in range(chunks):
        for pair in range(chunk * depth, (chunk + 1) * depth):
            turn(block, turned, pair)
        if chunk % 2 == 0:
            on_level(chunk, lambda copy: copy.start())
        arriving.append((
            send(0, chunk, turned, 3 - x_step, x_near),
            send(1, chunk, turned, 3 - y_step, y_near),
        ))
    own = pltpu.make_async_copy(turned, panels.at[3], own_sem)
    own.start()
    col_copies = share_with_peers(groups, block, shared, 1, col_send, col_recv)
    shared[0] = block[...]
    corner, spread = {}, {}
    lag = 2
    for chunk in range(chunks + lag):
        if chunk < chunks:
            by_y = chunk % 4 != 1
            arriving[chunk][0].wait_recv()
            if by_y:
                corner[chunk] = send(2, chunk, panels.at[3 + x_step], 3 + x_step - y_step, y_near)
            if chunk % 2 == 1:
                pass_on(0, chunk)
            arriving[chunk][1].wait_recv()
            if not by_y:
                corner[chunk] = send(2, chunk, panels.at[3 + y_step], 3 + y_step - x_step, x_near)
            if chunk % 2 == 1:
                pass_on(1, chunk)
            else:
                on_level(chunk, lambda copy: copy.wait_recv())
                late.append(from_held(3, chunk, x_held, 3 - x_step + 4 * x_sign, x_near))
                spread[chunk] = from_held(4, chunk, y_held, 3 - y_step + 4 * y_sign, y_near)
        done = chunk - lag
        if done >= 0:
            corner[done].wait_recv()
            if done % 2 == 1:
                pass_on(2, done)
            else:
                spread[done].wait_recv()
                slot = 3 + y_step - 4 * y_sign
                late.append(send(5, done, panels.at[slot], slot - x_step, x_near))
    for copy in late:
        copy.wait_recv()
    for chunk in range(0, chunks, 2):
        on_level(chunk, lambda copy: copy.wait_send())
    for copy in others:
        copy.wait_send()
    for copy in col_copies:
        copy.wait()
    own.wait()


def fetch(density, groups, size, span, planes):
    chunks = 8
    if planes:
        body, shape = functools.partial(relay_kernel, groups, size, chunks), (6, chunks)
    else:
        body, shape = functools.partial(direct_kernel, groups, size, span), (2 * span,)
    inside = pl.BlockSpec(memory_space=pltpu.VMEM)
    rows, width, depth = density.shape
    turned = (rows // 2, depth, 2 * width)
    extra = []
    if planes:
        extra = [
            pltpu.VMEM((2, chunks // 2, rows // 2 // chunks, depth, 2 * width), density.dtype),
            pltpu.SemaphoreType.DMA((2, chunks // 2)),
            pltpu.SemaphoreType.DMA((2, chunks // 2)),
        ]
    panels, shared = pl.pallas_call(
        body,
        in_specs=[inside],
        out_specs=[inside, inside],
        out_shape=[
            jax.ShapeDtypeStruct((2 * span + 1,) + turned, density.dtype),
            jax.ShapeDtypeStruct((groups,) + density.shape, density.dtype),
        ],
        scratch_shapes=[
            pltpu.VMEM(turned, density.dtype),
            pltpu.SemaphoreType.DMA,
            pltpu.SemaphoreType.DMA((groups - 1, PIECES)),
            pltpu.SemaphoreType.DMA((groups - 1, PIECES)),
            pltpu.SemaphoreType.DMA(shape),
            pltpu.SemaphoreType.DMA(shape),
        ] + extra,
        compiler_params=pltpu.CompilerParams(
            collective_id=0, has_side_effects=True, vmem_limit_bytes=LIMIT
        ),
    )(density)
    return panels.reshape((-1,) + turned[1:]), shared


def live_list(columns, rows, width, group_size, span):
    total, stored = columns.shape
    base = lax.axis_index("row") * rows
    first = lax.axis_index("col") * group_size
    own = lax.dynamic_slice_in_dim(columns, base, rows, 0)
    wanted = lax.dynamic_slice_in_dim(own, first, group_size, 1)
    group = lax.dynamic_slice_in_dim(columns, first, group_size, 1)
    candidates = jnp.take(group, own, axis=0)
    distance = jnp.mod(own - base + span * rows, total)
    equal = candidates[:, :, :, None] == wanted[:, None, None, :]
    slots = jnp.arange(group_size, dtype=jnp.int32)
    live = jnp.any(equal, axis=-1)
    place = jnp.sum(jnp.where(equal, slots, 0), axis=-1)
    inner = jnp.mod(jnp.arange(stored, dtype=jnp.int32) - first, stored)[None, :, None]
    odd = jnp.mod(inner, 2)
    flip = (jnp.mod(distance[:, :, None], 2) != odd).astype(jnp.int32)
    code = (distance[:, :, None] // 2) * 256 + slots
    code = (code * 256 + inner // 2) * 16 + place
    code = code * 4 + flip * 2 + odd
    length = stored * group_size // 2

    def by_parity(values):
        return values.reshape(rows, stored // 2, 2, group_size).transpose(0, 2, 1, 3).reshape(rows, 2, length)

    flat, code = by_parity(live), by_parity(code)
    order = jnp.cumsum(flat.astype(jnp.int32), axis=2)
    ranks = jnp.arange(1, length + 1, dtype=jnp.int32)
    wanted_rank = jnp.minimum(ranks, order[:, :, -1:])
    chosen = flat[:, :, None, :] & (order[:, :, None, :] == wanted_rank[:, :, :, None])
    packed = jnp.sum(jnp.where(chosen, code[:, :, None, :], 0), axis=-1)
    return order[:, :, -1].reshape(-1), packed.reshape(2 * rows, length)


def fill_halves(halves_ref, width):
    lane = lax.broadcasted_iota(jnp.int32, (width, 2 * width), 1)
    high = jnp.where(lane >= width, 1.0, 0.0)
    halves_ref[...] = jnp.zeros(halves_ref.shape, halves_ref.dtype)
    for flip in range(2):
        for odd in range(2):
            halves_ref[2 * flip + odd, flip] = (high if odd else 1.0 - high).astype(halves_ref.dtype)


def multiply(right_ref, left_refs):
    depth = left_refs[0].shape[-1]
    total, start = None, 0
    for left_ref in left_refs:
        part = lax.dot_general(
            right_ref[:, start:start + depth], left_ref[...], (((1,), (1,)), ((), ())),
            preferred_element_type=jnp.float32,
        )
        total = part if total is None else total + part
        start += depth
    return total.T


def first_kernel(stored, group_size, width, count_ref, code_ref, panels_ref, left_ref, rights, square_ref, halves_ref):
    rows, depth, _ = rights.shape
    fill_halves(halves_ref, width)

    def fill(row, carry):
        right_ref = rights.at[row]
        right_ref[...] = jnp.zeros(right_ref.shape, right_ref.dtype)
        assemble(count_ref, code_ref, panels_ref, halves_ref, row, right_ref, width)
        return carry

    def one_row(row, carry):
        total = multiply(rights.at[row], [left_ref.at[group, row] for group in range(left_ref.shape[0])])
        square_ref[row] = total.astype(square_ref.dtype)
        return carry

    lax.fori_loop(0, rows, fill, 0)
    lax.fori_loop(0, rows, one_row, 0, unroll=4)


def second_kernel(own_ref, shared_ref, rights, out_hbm, out_ref, out_sem):
    rows = own_ref.shape[0]

    def leave(row):
        return pltpu.make_async_copy(out_ref.at[row], out_hbm.at[row], out_sem.at[row])

    def one_row(row, carry):
        left = [own_ref.at[row]] + [shared_ref.at[step, row] for step in range(shared_ref.shape[0])]
        out_ref[row] = 3.0 * own_ref[row].astype(jnp.float32) - 2.0 * multiply(rights.at[row], left)
        leave(row).start()
        return carry

    def done(row, carry):
        leave(row).wait()
        return carry

    lax.fori_loop(0, rows, one_row, 0, unroll=4)
    lax.fori_loop(0, rows, done, 0)


def assemble(count_ref, code_ref, panels_ref, halves_ref, row, right_ref, width):
    for parity in range(2):
        line = 2 * row + parity

        def one(entry, carry):
            pieces = []
            for part in range(UNROLL):
                code = code_ref[line, entry * UNROLL + part]
                kind = code & 3
                place, inner = (code >> 2) & 15, (code >> 6) & 255
                slot, source = (code >> 14) & 255, code >> 22
                value = panels_ref[source, pl.ds(pl.multiple_of(slot * width, width), width), :]
                swapped = jnp.concatenate([value[:, width:], value[:, :width]], axis=1)
                value = value * halves_ref[kind, 0] + swapped * halves_ref[kind, 1]
                lanes = pl.ds(pl.multiple_of(inner * 2 * width, 2 * width), 2 * width)
                lines = pl.ds(pl.multiple_of(place * width, width), width)
                if parity == 1:
                    value = value + right_ref[lines, lanes]
                pieces.append((lines, lanes, value))
            for lines, lanes, value in pieces:
                right_ref[lines, lanes] = value
            return carry

        lax.fori_loop(0, lax.div(count_ref[line] + UNROLL - 1, UNROLL), one, 0)


def shards(density, columns):
    rows, width, depth = density.shape
    total, stored = columns.shape
    group_size = depth // width
    groups = stored // group_size
    span = -(-REACH // rows)
    count, codes = live_list(columns, rows, width, group_size, span)
    size = lax.axis_size("row")
    planes = (size, groups, span) == (16, 2, 3)
    panels, left = fetch(density, groups, size, span, planes)
    inside = pl.BlockSpec(memory_space=pltpu.VMEM)
    scalars = pl.BlockSpec(memory_space=pltpu.SMEM)
    right, square = pl.pallas_call(
        functools.partial(first_kernel, stored, group_size, width),
        in_specs=[scalars, scalars, inside, inside],
        out_specs=[inside, inside],
        out_shape=[
            jax.ShapeDtypeStruct((rows, depth, stored * width), density.dtype),
            jax.ShapeDtypeStruct(density.shape, density.dtype),
        ],
        scratch_shapes=[pltpu.VMEM((4, 2, width, 2 * width), density.dtype)],
        compiler_params=pltpu.CompilerParams(vmem_limit_bytes=LIMIT),
    )(count, codes, panels, left)
    return pl.pallas_call(
        second_kernel,
        in_specs=[inside, inside, inside],
        out_specs=pl.BlockSpec(memory_space=pl.ANY),
        out_shape=jax.ShapeDtypeStruct(density.shape, jnp.float32),
        scratch_shapes=[
            pltpu.VMEM(density.shape, jnp.float32),
            pltpu.SemaphoreType.DMA((rows,)),
        ],
        compiler_params=pltpu.CompilerParams(vmem_limit_bytes=LIMIT),
    )(square, exchange(square, groups, 1), right)


def solution(mesh):
    placed = (P("row", None, "col"), P())
    return jax.shard_map(
        shards, mesh=mesh, in_specs=placed, out_specs=P("row", None, "col"), check_vma=False
    )
```

```python
import functools

import jax
import jax.numpy as jnp
from jax import lax
from jax.experimental import pallas as pl
from jax.experimental.pallas import tpu as pltpu
from jax.sharding import PartitionSpec as P

REACH = 48
UNROLL = 8
PIECES = 8
LIMIT = 8 * 1024 * 1024


def greet(devices):
    barrier = pltpu.get_barrier_semaphore()
    for device in devices:
        pl.semaphore_signal(barrier, inc=1, device_id=device, device_id_type=pl.DeviceIdType.MESH)
    pl.semaphore_wait(barrier, len(devices))


def col_peers(groups):
    return [{"col": lax.rem(lax.axis_index("col") + step, groups)} for step in range(1, groups)]


def share_with_peers(groups, block, shared, first, send_sem, recv_sem):
    copies = []
    chunks = send_sem.shape[1]
    depth = block.shape[0] // chunks
    for step, peer in enumerate(col_peers(groups)):
        for chunk in range(chunks):
            lines = pl.ds(chunk * depth, depth)
            copies.append(pltpu.make_async_remote_copy(
                src_ref=block.at[lines], dst_ref=shared.at[first + groups - 2 - step, lines],
                send_sem=send_sem.at[step, chunk], recv_sem=recv_sem.at[step, chunk],
                device_id=peer, device_id_type=pl.DeviceIdType.MESH,
            ))
            copies[-1].start()
    return copies


def exchange_kernel(groups, block, shared, send_sem, recv_sem):
    greet(col_peers(groups))
    for copy in share_with_peers(groups, block, shared, 0, send_sem, recv_sem):
        copy.wait()


def exchange(block, groups, collective_id):
    return pl.pallas_call(
        functools.partial(exchange_kernel, groups),
        in_specs=[pl.BlockSpec(memory_space=pltpu.VMEM)],
        out_specs=pl.BlockSpec(memory_space=pltpu.VMEM),
        out_shape=jax.ShapeDtypeStruct((groups - 1,) + block.shape, block.dtype),
        scratch_shapes=[pltpu.SemaphoreType.DMA((groups - 1, PIECES))] * 2,
        compiler_params=pltpu.CompilerParams(
            collective_id=collective_id, has_side_effects=True, vmem_limit_bytes=LIMIT
        ),
    )(block)


def turn(block, turned, pair):
    wide = jnp.concatenate([block[2 * pair], block[2 * pair + 1]], axis=0)
    turned[pair] = wide.T


def direct_kernel(groups, size, span, block, panels, shared, turned, own_sem, col_send, col_recv, send_sem, recv_sem):
    me = lax.axis_index("row")
    offsets = [d for d in range(-span, span + 1) if d != 0]
    greet([{"row": lax.rem(me + d + size, size)} for d in offsets] + col_peers(groups))
    copies = share_with_peers(groups, block, shared, 1, col_send, col_recv)
    shared[0] = block[...]
    for pair in range(turned.shape[0]):
        turn(block, turned, pair)
    own = pltpu.make_async_copy(turned, panels.at[span], own_sem)
    own.start()
    for step, d in enumerate(offsets):
        copies.append(pltpu.make_async_remote_copy(
            src_ref=turned, dst_ref=panels.at[span - d], send_sem=send_sem.at[step], recv_sem=recv_sem.at[step],
            device_id={"row": lax.rem(me + d + size, size)}, device_id_type=pl.DeviceIdType.MESH,
        ))
        copies[-1].start()
    for copy in copies:
        copy.wait()
    own.wait()


def relay_kernel(groups, size, chunks, block, panels, shared, turned, own_sem, col_send, col_recv, send_sem, recv_sem, held, up_send, up_recv):
    me = lax.axis_index("row")
    x_step = 1 - 2 * lax.rem(me, 2)
    y_step = 2 - 4 * lax.rem(lax.div(me, 2), 2)
    steps = [x_step, y_step, x_step + y_step]
    x_near, y_near = me + x_step, me + y_step
    above, below = lax.rem(me + 4, size), lax.rem(me + size - 4, size)
    greet([{"row": d} for d in (x_near, y_near, above, below)] + col_peers(groups))
    others = []
    depth = turned.shape[0] // chunks

    def send(kind, chunk, source, slot, device):
        lines = pl.ds(chunk * depth, depth)
        copy = pltpu.make_async_remote_copy(
            src_ref=source.at[lines], dst_ref=panels.at[slot, lines],
            send_sem=send_sem.at[kind, chunk], recv_sem=recv_sem.at[kind, chunk],
            device_id={"row": device}, device_id_type=pl.DeviceIdType.MESH,
        )
        copy.start()
        others.append(copy)
        return copy

    def from_held(kind, chunk, way, slot, device):
        lines = pl.ds(chunk * depth, depth)
        copy = pltpu.make_async_remote_copy(
            src_ref=held.at[way, chunk // 2], dst_ref=panels.at[slot, lines],
            send_sem=send_sem.at[kind, chunk], recv_sem=recv_sem.at[kind, chunk],
            device_id={"row": device}, device_id_type=pl.DeviceIdType.MESH,
        )
        copy.start()
        others.append(copy)
        return copy

    def pass_on(kind, chunk):
        step = steps[kind]
        sign = jnp.where(step > 0, 1, -1)
        target = lax.rem(me + 4 * sign + size, size)
        late.append(send(3 + kind, chunk, panels.at[3 + step], 3 + step - 4 * sign, target))

    place = lax.rem(me, 4)
    x_sign, y_sign = x_step, lax.div(y_step, 2)
    x_held = lax.div(1 + x_sign, 2)
    y_held = lax.div(1 + y_sign, 2)

    def level(way, chunk):
        lines = pl.ds(chunk * depth, depth)
        return pltpu.make_async_remote_copy(
            src_ref=turned.at[lines], dst_ref=held.at[way, chunk // 2],
            send_sem=up_send.at[way, chunk // 2], recv_sem=up_recv.at[way, chunk // 2],
            device_id={"row": above if way == 0 else below}, device_id_type=pl.DeviceIdType.MESH,
        )

    def on_level(chunk, act):
        @pl.when(place > 0)
        def _():
            act(level(0, chunk))

        @pl.when(place < 3)
        def _():
            act(level(1, chunk))

    late, arriving = [], []
    for chunk in range(chunks):
        for pair in range(chunk * depth, (chunk + 1) * depth):
            turn(block, turned, pair)
        if chunk % 2 == 0:
            on_level(chunk, lambda copy: copy.start())
        arriving.append((
            send(0, chunk, turned, 3 - x_step, x_near),
            send(1, chunk, turned, 3 - y_step, y_near),
        ))
    own = pltpu.make_async_copy(turned, panels.at[3], own_sem)
    own.start()
    col_copies = share_with_peers(groups, block, shared, 1, col_send, col_recv)
    shared[0] = block[...]
    corner, spread = {}, {}
    lag = 2
    for chunk in range(chunks + lag):
        if chunk < chunks:
            by_y = chunk % 4 != 1
            arriving[chunk][0].wait_recv()
            if by_y:
                corner[chunk] = send(2, chunk, panels.at[3 + x_step], 3 + x_step - y_step, y_near)
            if chunk % 2 == 1:
                pass_on(0, chunk)
            arriving[chunk][1].wait_recv()
            if not by_y:
                corner[chunk] = send(2, chunk, panels.at[3 + y_step], 3 + y_step - x_step, x_near)
            if chunk % 2 == 1:
                pass_on(1, chunk)
            else:
                on_level(chunk, lambda copy: copy.wait_recv())
                late.append(from_held(3, chunk, x_held, 3 - x_step + 4 * x_sign, x_near))
                spread[chunk] = from_held(4, chunk, y_held, 3 - y_step + 4 * y_sign, y_near)
        done = chunk - lag
        if done >= 0:
            corner[done].wait_recv()
            if done % 2 == 1:
                pass_on(2, done)
            else:
                spread[done].wait_recv()
                slot = 3 + y_step - 4 * y_sign
                late.append(send(5, done, panels.at[slot], slot - x_step, x_near))
    for copy in late:
        copy.wait_recv()
    for chunk in range(0, chunks, 2):
        on_level(chunk, lambda copy: copy.wait_send())
    for copy in others:
        copy.wait_send()
    for copy in col_copies:
        copy.wait()
    own.wait()


def fetch(density, groups, size, span, planes):
    chunks = 8
    if planes:
        body, shape = functools.partial(relay_kernel, groups, size, chunks), (6, chunks)
    else:
        body, shape = functools.partial(direct_kernel, groups, size, span), (2 * span,)
    inside = pl.BlockSpec(memory_space=pltpu.VMEM)
    rows, width, depth = density.shape
    turned = (rows // 2, depth, 2 * width)
    extra = []
    if planes:
        extra = [
            pltpu.VMEM((2, chunks // 2, rows // 2 // chunks, depth, 2 * width), density.dtype),
            pltpu.SemaphoreType.DMA((2, chunks // 2)),
            pltpu.SemaphoreType.DMA((2, chunks // 2)),
        ]
    panels, shared = pl.pallas_call(
        body,
        in_specs=[inside],
        out_specs=[inside, inside],
        out_shape=[
            jax.ShapeDtypeStruct((2 * span + 1,) + turned, density.dtype),
            jax.ShapeDtypeStruct((groups,) + density.shape, density.dtype),
        ],
        scratch_shapes=[
            pltpu.VMEM(turned, density.dtype),
            pltpu.SemaphoreType.DMA,
            pltpu.SemaphoreType.DMA((groups - 1, PIECES)),
            pltpu.SemaphoreType.DMA((groups - 1, PIECES)),
            pltpu.SemaphoreType.DMA(shape),
            pltpu.SemaphoreType.DMA(shape),
        ] + extra,
        compiler_params=pltpu.CompilerParams(
            collective_id=0, has_side_effects=True, vmem_limit_bytes=LIMIT
        ),
    )(density)
    return panels.reshape((-1,) + turned[1:]), shared


def live_list(columns, rows, width, group_size, span):
    total, stored = columns.shape
    base = lax.axis_index("row") * rows
    first = lax.axis_index("col") * group_size
    own = lax.dynamic_slice_in_dim(columns, base, rows, 0)
    wanted = lax.dynamic_slice_in_dim(own, first, group_size, 1)
    group = lax.dynamic_slice_in_dim(columns, first, group_size, 1)
    candidates = jnp.take(group, own, axis=0)
    distance = jnp.mod(own - base + span * rows, total)
    equal = candidates[:, :, :, None] == wanted[:, None, None, :]
    slots = jnp.arange(group_size, dtype=jnp.int32)
    live = jnp.any(equal, axis=-1)
    place = jnp.sum(jnp.where(equal, slots, 0), axis=-1)
    inner = jnp.mod(jnp.arange(stored, dtype=jnp.int32) - first, stored)[None, :, None]
    odd = jnp.mod(inner, 2)
    flip = (jnp.mod(distance[:, :, None], 2) != odd).astype(jnp.int32)
    code = (distance[:, :, None] // 2) * 256 + slots
    code = (code * 256 + inner // 2) * 16 + place
    code = code * 4 + flip * 2 + odd
    length = stored * group_size // 2

    def by_parity(values):
        return values.reshape(rows, stored // 2, 2, group_size).transpose(0, 2, 1, 3).reshape(rows, 2, length)

    flat, code = by_parity(live), by_parity(code)
    order = jnp.cumsum(flat.astype(jnp.int32), axis=2)
    ranks = jnp.arange(1, length + 1, dtype=jnp.int32)
    wanted_rank = jnp.minimum(ranks, order[:, :, -1:])
    chosen = flat[:, :, None, :] & (order[:, :, None, :] == wanted_rank[:, :, :, None])
    packed = jnp.sum(jnp.where(chosen, code[:, :, None, :], 0), axis=-1)
    return order[:, :, -1].reshape(-1), packed.reshape(2 * rows, length)


def fill_halves(halves_ref, width):
    lane = lax.broadcasted_iota(jnp.int32, (width, 2 * width), 1)
    high = jnp.where(lane >= width, 1.0, 0.0)
    halves_ref[...] = jnp.zeros(halves_ref.shape, halves_ref.dtype)
    for flip in range(2):
        for odd in range(2):
            halves_ref[2 * flip + odd, flip] = (high if odd else 1.0 - high).astype(halves_ref.dtype)


def multiply(right_ref, left_refs):
    depth = left_refs[0].shape[-1]
    total, start = None, 0
    for left_ref in left_refs:
        part = lax.dot_general(
            right_ref[:, start:start + depth], left_ref[...], (((1,), (1,)), ((), ())),
            preferred_element_type=jnp.float32,
        )
        total = part if total is None else total + part
        start += depth
    return total.T


def first_kernel(stored, group_size, width, count_ref, code_ref, panels_ref, left_ref, rights, square_ref, halves_ref):
    rows, depth, _ = rights.shape
    fill_halves(halves_ref, width)

    def fill(row, carry):
        right_ref = rights.at[row]
        right_ref[...] = jnp.zeros(right_ref.shape, right_ref.dtype)
        assemble(count_ref, code_ref, panels_ref, halves_ref, row, right_ref, width)
        return carry

    def one_row(row, carry):
        total = multiply(rights.at[row], [left_ref.at[group, row] for group in range(left_ref.shape[0])])
        square_ref[row] = total.astype(square_ref.dtype)
        return carry

    lax.fori_loop(0, rows, fill, 0)
    lax.fori_loop(0, rows, one_row, 0, unroll=4)


def second_kernel(own_ref, shared_ref, rights, out_hbm, out_ref, out_sem):
    rows = own_ref.shape[0]

    def leave(row):
        return pltpu.make_async_copy(out_ref.at[row], out_hbm.at[row], out_sem.at[row])

    def one_row(row, carry):
        left = [own_ref.at[row]] + [shared_ref.at[step, row] for step in range(shared_ref.shape[0])]
        out_ref[row] = 3.0 * own_ref[row].astype(jnp.float32) - 2.0 * multiply(rights.at[row], left)
        leave(row).start()
        return carry

    def done(row, carry):
        leave(row).wait()
        return carry

    lax.fori_loop(0, rows, one_row, 0, unroll=4)
    lax.fori_loop(0, rows, done, 0)


def assemble(count_ref, code_ref, panels_ref, halves_ref, row, right_ref, width):
    for parity in range(2):
        line = 2 * row + parity

        def one(entry, carry):
            pieces = []
            for part in range(UNROLL):
                code = code_ref[line, entry * UNROLL + part]
                kind = code & 3
                place, inner = (code >> 2) & 15, (code >> 6) & 255
                slot, source = (code >> 14) & 255, code >> 22
                value = panels_ref[source, pl.ds(pl.multiple_of(slot * width, width), width), :]
                swapped = pltpu.roll(value, width, 1)
                value = value * halves_ref[kind, 0] + swapped * halves_ref[kind, 1]
                lanes = pl.ds(pl.multiple_of(inner * 2 * width, 2 * width), 2 * width)
                lines = pl.ds(pl.multiple_of(place * width, width), width)
                if parity == 1:
                    value = value + right_ref[lines, lanes]
                pieces.append((lines, lanes, value))
            for lines, lanes, value in pieces:
                right_ref[lines, lanes] = value
            return carry

        lax.fori_loop(0, lax.div(count_ref[line] + UNROLL - 1, UNROLL), one, 0)


def shards(density, columns):
    rows, width, depth = density.shape
    total, stored = columns.shape
    group_size = depth // width
    groups = stored // group_size
    span = -(-REACH // rows)
    count, codes = live_list(columns, rows, width, group_size, span)
    size = lax.axis_size("row")
    planes = (size, groups, span) == (16, 2, 3)
    panels, left = fetch(density, groups, size, span, planes)
    inside = pl.BlockSpec(memory_space=pltpu.VMEM)
    scalars = pl.BlockSpec(memory_space=pltpu.SMEM)
    right, square = pl.pallas_call(
        functools.partial(first_kernel, stored, group_size, width),
        in_specs=[scalars, scalars, inside, inside],
        out_specs=[inside, inside],
        out_shape=[
            jax.ShapeDtypeStruct((rows, depth, stored * width), density.dtype),
            jax.ShapeDtypeStruct(density.shape, density.dtype),
        ],
        scratch_shapes=[pltpu.VMEM((4, 2, width, 2 * width), density.dtype)],
        compiler_params=pltpu.CompilerParams(vmem_limit_bytes=LIMIT),
    )(count, codes, panels, left)
    return pl.pallas_call(
        second_kernel,
        in_specs=[inside, inside, inside],
        out_specs=pl.BlockSpec(memory_space=pl.ANY),
        out_shape=jax.ShapeDtypeStruct(density.shape, jnp.float32),
        scratch_shapes=[
            pltpu.VMEM(density.shape, jnp.float32),
            pltpu.SemaphoreType.DMA((rows,)),
        ],
        compiler_params=pltpu.CompilerParams(vmem_limit_bytes=LIMIT),
    )(square, exchange(square, groups, 1), right)


def solution(mesh):
    placed = (P("row", None, "col"), P())
    return jax.shard_map(
        shards, mesh=mesh, in_specs=placed, out_specs=P("row", None, "col"), check_vma=False
    )
```
